512 devices in a mesh: blk: 32 (over x, z_lo, core), dp: 16 (over y, z_hi).
Axes of the slice: x: 4, y: 8, z: 8 (z_hi: 2, z_lo: 4; z = z_hi * 4 + z_lo), core: 2. Of those that a mesh axis runs over, the one named last changes fastest.
Arguments:
- inputs: bfloat16 [4096, 2560], P('blk'), may hold values from -400 to 400
- gain: float32 [2560], replicated, may hold values from 0.1 to 1.9
- w_gate: bfloat16 [2560, 6912], P('blk', 'dp'), may hold values from -0.125 to 0.125
- w_up: bfloat16 [2560, 6912], P('blk', 'dp'), may hold values from -0.125 to 0.125
- upstream: bfloat16 [4096, 6912], P('blk', 'dp'), may hold values from -6 to 6
Outputs:
- hidden: bfloat16 [4096, 6912], P('blk', 'dp')
- grad_gate: float32 [2560, 6912], P('blk', 'dp')
- grad_up: float32 [2560, 6912], P('blk', 'dp')
- grad_input: bfloat16 [4096, 2560], P('blk', 'dp')
- grad_gain: float32 [2560], P('dp')
The draws below stay inside these ranges and needn't reach their ends.
All inputs are finite; a program needn't handle non-finite values.
Results may differ from the reference program's by a relative error of at most 0.028.
Values may be sent and summed in bfloat16 or wider, within the bound.
No kernel may reach another device: no remote copies, remote signals or barrier semaphores. Data moves between devices by JAX's collectives and lax.ppermute only.
A program may use at most 64 MiB of HBM per device.

```python
import math
import jax
import jax.numpy as jnp
from jax import lax

D = 2560
FF_WIN = 6912
TOKENS = 4096
N_DP = 16


def draw_inputs(key, part):
    key = jax.random.fold_in(key, 11)
    base_key, row_key, col_key = jax.random.split(key, 3)
    row_scale = jnp.exp(jax.random.uniform(row_key, (TOKENS, 1), jnp.float32) * math.log(10.0))
    col_scale = jnp.exp(jax.random.uniform(col_key, (1, D), jnp.float32) * math.log(10.0))
    base = jnp.clip(jax.random.normal(base_key, (TOKENS, D), jnp.float32), -3.9, 3.9)
    return (base * row_scale * col_scale).astype(jnp.bfloat16)


def shard_levels(own_key, extent, cuts, low, high):
    level = 1.0
    for position, parts in cuts:
        draws = jax.random.uniform(jax.random.fold_in(jax.random.fold_in(own_key, 6), position), (parts,), jnp.float32, low / len(cuts), high / len(cuts))
        level = level * jnp.repeat(jnp.exp(draws), extent[position] // parts).reshape((-1,) + (1,) * (len(extent) - 1 - position))
    return level


def normal_values(key, extent, width, most, cuts=(), dtype=jnp.bfloat16):
    result = width * jax.random.normal(key, extent, jnp.float32)
    if cuts:
        result = result * shard_levels(key, extent, cuts, -0.22, 0.18)
    return jnp.clip(result, -most, most).astype(dtype)


def setup_inputs(seed: int = 0) -> dict:
    keys = jax.random.split(jax.random.key(seed), 6)
    return {
        "inputs": draw_inputs(jax.random.fold_in(keys[5], 71), 0),
        "gain": jnp.clip(1.0 + 0.18 * jax.random.normal(keys[1], (D,), jnp.float32), 0.1, 1.9),
        "w_gate": normal_values(keys[2], (D, FF_WIN), D ** -0.5, 0.125, ((0, 32), (1, 16))),
        "w_up": normal_values(keys[3], (D, FF_WIN), D ** -0.5, 0.125, ((0, 32), (1, 16))),
        "upstream": normal_values(keys[4], (TOKENS, FF_WIN), 1.0, 6.0, ((0, 32), (1, 16))),
    }


def reference(inputs, gain, w_gate, w_up, upstream):
    wide_input = inputs.astype(jnp.float32)
    root_mean = jnp.sqrt(lax.optimization_barrier(jnp.mean(wide_input * wide_input, axis=1, keepdims=True)) + 1e-05)
    unit_input = wide_input / root_mean
    normed = (unit_input * gain).astype(jnp.bfloat16)
    gate_pre = jnp.dot(normed, w_gate, preferred_element_type=jnp.float32)
    up_pre = jnp.dot(normed, w_up, preferred_element_type=jnp.float32)
    sigmoid_gate = jax.nn.sigmoid(gate_pre)
    activated = gate_pre * sigmoid_gate
    hidden = (activated * up_pre).astype(jnp.bfloat16)
    upstream_wide = upstream.astype(jnp.float32)
    back_up = (upstream_wide * activated).astype(jnp.bfloat16)
    back_gate = (upstream_wide * up_pre * sigmoid_gate * (1.0 + gate_pre * (1.0 - sigmoid_gate))).astype(jnp.bfloat16)
    grad_gate = jnp.dot(normed.T, back_gate, preferred_element_type=jnp.float32)
    grad_up = jnp.dot(normed.T, back_up, preferred_element_type=jnp.float32)
    group_cols = w_gate.shape[1] // N_DP
    back_normed = jnp.zeros((inputs.shape[0], inputs.shape[1]), jnp.float32)
    for group in range(N_DP):
        lower = group * group_cols
        upper = lower + group_cols
        group_part = jnp.dot(back_gate[:, lower:upper], w_gate[:, lower:upper].T, preferred_element_type=jnp.float32) + jnp.dot(back_up[:, lower:upper], w_up[:, lower:upper].T, preferred_element_type=jnp.float32)
        rounded = lax.optimization_barrier(group_part.astype(jnp.bfloat16))
        back_normed = back_normed + rounded.astype(jnp.float32)
    token_dots = lax.optimization_barrier(jnp.sum(back_normed * gain * unit_input, axis=1, keepdims=True))
    grad_input = ((back_normed * gain - unit_input * token_dots / inputs.shape[1]) / root_mean).astype(jnp.bfloat16)
    grad_gain = lax.optimization_barrier(jnp.sum(back_normed * unit_input, axis=0))
    return (hidden, grad_gate, grad_up, grad_input, grad_gain)
```

```python
import jax
import jax.numpy as jnp
from jax import lax
from jax.sharding import PartitionSpec as P

BF = jnp.bfloat16
F32 = jnp.float32
NX, NZ, NC = 4, 4, 2


def place(x, z, c):
    return (x * NZ + z) * NC + c


def pairs(move):
    return [
        (place(x, z, c), place(*move(x, z, c)))
        for x in range(NX)
        for z in range(NZ)
        for c in range(NC)
    ]


def swap_core(value):
    return lax.ppermute(value, "blk", pairs(lambda x, z, c: (x, z, 1 - c)))


def shift_x(value, steps):
    return lax.ppermute(value, "blk", pairs(lambda x, z, c: ((x + steps) % NX, z, c)))


X_GROUPS = [[place(x, z, c) for x in range(NX)] for z in range(NZ) for c in range(NC)]
Z_GROUPS = [[place(x, z, c) for z in range(NZ)] for x in range(NX) for c in range(NC)]


def per_device(inputs, gain, w_gate, w_up, upstream):
    position = lax.axis_index("blk")
    core = position % NC
    x_place = position // (NZ * NC)
    first = core == 0
    tokens, width = inputs.shape
    rows, columns = w_gate.shape
    half = columns // 2
    n_dp = lax.axis_size("dp")
    features = width // n_dp

    def ordered(own, other, axis):
        return jnp.where(
            first, jnp.concatenate([own, other], axis), jnp.concatenate([other, own], axis)
        )

    def halves(value):
        low, high = value[:, :half], value[:, half:]
        return jnp.where(first, low, high), jnp.where(first, high, low)

    gate_mine, gate_other = halves(w_gate)
    up_mine, up_other = halves(w_up)
    weight_other = swap_core(jnp.concatenate([gate_other, up_other], 1))
    weight_mine = jnp.concatenate([gate_mine, up_mine], 1)
    weight_chip = ordered(weight_mine, weight_other, 0)
    upstream_mine, upstream_other = halves(upstream)
    upstream_pair = jnp.concatenate([upstream_mine, swap_core(upstream_other)], 0)
    inputs_pair = jnp.concatenate([inputs, swap_core(inputs)], 0)

    wide_input = inputs_pair.astype(F32)
    root_mean = jnp.sqrt(jnp.mean(wide_input * wide_input, axis=1, keepdims=True) + 1e-05)
    normed = (wide_input / root_mean * gain).astype(BF)

    column = lax.all_gather(weight_chip, "blk", axis=0, tiled=True, axis_index_groups=Z_GROUPS)
    weight = lax.all_gather(column, "blk", axis=0, tiled=True, axis_index_groups=X_GROUPS)

    pre = jnp.dot(normed, weight, preferred_element_type=F32)
    gate_pre, up_pre = pre[:, :half], pre[:, half:]
    sigmoid_gate = jax.nn.sigmoid(gate_pre)
    activated = gate_pre * sigmoid_gate
    hidden_pair = (activated * up_pre).astype(BF)
    upstream_wide = upstream_pair.astype(F32)
    back_up = (upstream_wide * activated).astype(BF)
    back_gate = (
        upstream_wide * up_pre * sigmoid_gate * (1.0 + gate_pre * (1.0 - sigmoid_gate))
    ).astype(BF)
    back = jnp.concatenate([back_gate, back_up], 1)

    part = lax.dot_general(
        weight, back, (((1,), (1,)), ((), ())), preferred_element_type=F32
    )
    part_other = swap_core(part[:, tokens:].astype(BF))
    hidden_other = swap_core(hidden_pair[tokens:])
    hidden = ordered(hidden_pair[:tokens], hidden_other, 1)

    def term(steps):
        size = rows * NZ * NC
        block = lax.dynamic_slice_in_dim(normed, ((x_place + steps) % NX) * size, size, 1)
        return lax.dot_general(block, back, (((0,), (0,)), ((), ())), preferred_element_type=F32)

    travelling = [shift_x(term(steps).astype(BF), steps) for steps in (2, 1, 3)]

    unit_t = (wide_input[:tokens] / root_mean[:tokens]).T
    group_part = (part[:, :tokens] + part_other.astype(F32)).astype(BF)
    dots = jnp.sum(group_part.astype(F32) * gain[:, None] * unit_t, axis=0)
    dots_high = dots.astype(BF)
    rest = dots - dots_high.astype(F32)
    dots_mid = rest.astype(BF)
    dots_low = (rest - dots_mid.astype(F32)).astype(BF)
    dots_rows = jnp.stack([dots_high, dots_mid, dots_low], 0)
    dots_rows = jnp.pad(dots_rows, ((0, 13), (0, 0)))
    sending = jnp.concatenate(
        [
            group_part.reshape(n_dp, features, tokens),
            jnp.broadcast_to(dots_rows, (n_dp,) + dots_rows.shape),
        ],
        1,
    )
    got = lax.all_to_all(sending, "dp", 0, 0, tiled=True)
    totals = jnp.sum(got.astype(F32), axis=0)
    own_sums = totals[:features]
    token_totals = totals[features] + totals[features + 1] + totals[features + 2]

    start = lax.axis_index("dp") * features
    gain_slice = lax.dynamic_slice_in_dim(gain, start, features, 0)[:, None]
    unit_slice = lax.dynamic_slice_in_dim(unit_t, start, features, 0)
    grad_input = (
        (own_sums * gain_slice - unit_slice * (token_totals / width)[None, :])
        / root_mean[:tokens, 0][None, :]
    ).astype(BF).T
    gain_part = jnp.sum(own_sums * unit_slice, axis=1)
    gain_part = lax.psum(gain_part, "blk", axis_index_groups=X_GROUPS)
    gain_part = lax.psum(gain_part, "blk", axis_index_groups=Z_GROUPS)
    grad_gain = gain_part + swap_core(gain_part)

    column_sum = term(0)
    for value in travelling:
        column_sum = column_sum + value.astype(F32)
    blocks = column_sum.astype(BF).reshape(NZ, rows * NC, 2 * half)
    blocks = lax.all_to_all(blocks, "blk", 0, 0, tiled=True, axis_index_groups=Z_GROUPS)
    chip_sum = jnp.sum(blocks.astype(F32), axis=0)
    sum_mine = jnp.where(first, chip_sum[:rows], chip_sum[rows:])
    sum_other = swap_core(jnp.where(first, chip_sum[rows:], chip_sum[:rows]))
    grad_gate = ordered(sum_mine[:, :half], sum_other[:, :half], 1)
    grad_up = ordered(sum_mine[:, half:], sum_other[:, half:], 1)
    return (hidden, grad_gate, grad_up, grad_input, grad_gain)


def solution(mesh):
    return jax.shard_map(
        per_device,
        mesh=mesh,
        in_specs=(P("blk", None), P(), P("blk", "dp"), P("blk", "dp"), P("blk", "dp")),
        out_specs=(P("blk", "dp"), P("blk", "dp"), P("blk", "dp"), P("blk", "dp"), P("dp")),
        check_vma=False,
    )
```

```python
import jax
import jax.numpy as jnp
from jax import lax
from jax.experimental import pallas as pl
from jax.experimental.pallas import tpu as pltpu
from jax.sharding import PartitionSpec as P

BF = jnp.bfloat16
F32 = jnp.float32
NX, NZ, NC = 4, 4, 2
VMEM = pl.BlockSpec(memory_space=pltpu.VMEM)
SMEM = pl.BlockSpec(memory_space=pltpu.SMEM)
PARAMS = pltpu.CompilerParams(vmem_limit_bytes=48 * 1024 * 1024)
NT = (((1,), (1,)), ((), ()))
TN = (((0,), (0,)), ((), ()))


def place(x, z, c):
    return (x * NZ + z) * NC + c


def pairs(move):
    return [
        (place(x, z, c), place(*move(x, z, c)))
        for x in range(NX)
        for z in range(NZ)
        for c in range(NC)
    ]


def swap_core(value):
    return lax.ppermute(value, "blk", pairs(lambda x, z, c: (x, z, 1 - c)))


def shift_x(value, steps):
    return lax.ppermute(value, "blk", pairs(lambda x, z, c: ((x + steps) % NX, z, c)))


def shift_z(value, steps):
    return lax.ppermute(value, "blk", pairs(lambda x, z, c: (x, (z + steps) % NZ, c)))


X_GROUPS = [[place(x, z, c) for x in range(NX)] for z in range(NZ) for c in range(NC)]
Z_GROUPS = [[place(x, z, c) for z in range(NZ)] for x in range(NX) for c in range(NC)]


def block_order(spot_ref, index):
    return ((spot_ref[0] + index // NZ) % NX) * NZ + (spot_ref[1] + index % NZ) % NZ


def norm_kernel(spot_ref, x_ref, gain_ref, normed_ref, root_ref):
    width, tokens = x_ref.shape
    size = width // (NX * NZ)
    total = jnp.zeros((size, tokens), F32)
    for index in range(NX * NZ):
        value = x_ref[pl.ds(index * size, size), :].astype(F32)
        total += value * value
    root = jnp.sqrt(jnp.sum(total, axis=0, keepdims=True) / width + 1e-05)
    root_ref[...] = root
    for index in range(NX * NZ):
        rows = pl.ds(pl.multiple_of(block_order(spot_ref, index) * size, size), size)
        unit = x_ref[rows, :].astype(F32) / root
        gain = gain_ref[rows, :]
        gain = jnp.concatenate([gain, gain], axis=1)
        normed_ref[pl.ds(index * size, size), :] = (unit * gain).astype(BF)


def forward_kernel(normed_ref, upstream_ref, *refs):
    gates, ups = refs[:NX], refs[NX : 2 * NX]
    hidden_ref, back_ref, own_ref, other_ref = refs[2 * NX :]
    size = gates[0].shape[1]
    tokens = own_ref.shape[1]

    def product(pieces):
        total = None
        for index in range(NX):
            term = jnp.dot(
                pieces[index][...],
                normed_ref[pl.ds(index * size, size), :],
                preferred_element_type=F32,
            )
            total = term if total is None else total + term
        return total

    gate_pre = product(gates)
    up_pre = product(ups)
    sigmoid = 1.0 / (1.0 + jnp.exp(-gate_pre))
    activated = gate_pre * sigmoid
    hidden_ref[...] = (activated * up_pre).astype(BF)
    upstream = upstream_ref[...].astype(F32)
    back_up = (upstream * activated).astype(BF)
    back_gate = (upstream * up_pre * sigmoid * (1.0 + gate_pre * (1.0 - sigmoid))).astype(BF)
    back_ref[0] = back_gate
    back_ref[1] = back_up
    for index in range(NX):
        part = lax.dot_general(gates[index][...], back_gate, TN, preferred_element_type=F32)
        part += lax.dot_general(ups[index][...], back_up, TN, preferred_element_type=F32)
        rows = pl.ds(index * size, size)
        own_ref[rows, :] = part[:, :tokens]
        other_ref[rows, :] = part[:, tokens:].astype(BF)


def gradient_kernel(normed_ref, back_ref, *outs):
    size = outs[0].shape[2]
    for index in range(NX):
        rows = normed_ref[pl.ds(index * size, size), :]
        for which in range(2):
            term = lax.dot_general(back_ref[which], rows, NT, preferred_element_type=F32)
            outs[index][which] = term.astype(outs[index].dtype)


def blocks_kernel(spot_ref, own_ref, other_ref, x_ref, root_ref, gain_ref, out_ref):
    width, tokens = own_ref.shape
    size = width // (NX * NZ)
    root = root_ref[...]
    total = jnp.zeros((size, tokens), F32)
    for index in range(NX * NZ):
        here = pl.ds(index * size, size)
        block = block_order(spot_ref, index)
        rows = pl.ds(pl.multiple_of(block * size, size), size)
        part = (own_ref[here, :] + other_ref[here, :].astype(F32)).astype(BF)
        out_ref[block, 0:size, :] = part
        unit = x_ref[rows, :].astype(F32) / root
        total += part.astype(F32) * gain_ref[rows, :] * unit
    dots = jnp.sum(total, axis=0, keepdims=True)
    high = dots.astype(BF).astype(F32)
    mid = (dots - high).astype(BF).astype(F32)
    low = dots - high - mid
    spare = out_ref.shape[1] - size
    line = lax.broadcasted_iota(jnp.int32, (spare, tokens), 0)
    rows = jnp.where(line == 0, high, jnp.where(line == 1, mid, jnp.where(line == 2, low, 0.0)))
    for index in range(NX * NZ):
        out_ref[index, size : size + spare, :] = rows.astype(BF)


def call(kernel, outs, specs):
    return pl.pallas_call(
        kernel,
        out_shape=outs,
        in_specs=specs,
        out_specs=jax.tree.map(lambda _: VMEM, outs),
        compiler_params=PARAMS,
    )


def shape(dims, dtype):
    return jax.ShapeDtypeStruct(dims, dtype)


def per_device(inputs, gain, w_gate, w_up, upstream):
    position = lax.axis_index("blk")
    core = position % NC
    spot = jnp.stack([position // (NZ * NC), (position // NC) % NZ]).astype(jnp.int32)
    first = core == 0
    tokens, width = inputs.shape
    rows, columns = w_gate.shape
    half = columns // 2
    n_dp = lax.axis_size("dp")
    features = width // n_dp
    column_rows = rows * NZ * NC

    def ordered(own, other, axis):
        return jnp.where(
            first, jnp.concatenate([own, other], axis), jnp.concatenate([other, own], axis)
        )

    def halves(value, axis):
        low, high = jnp.split(value, 2, axis)
        return jnp.where(first, low, high), jnp.where(first, high, low)

    gate_mine, gate_other = halves(w_gate, 1)
    up_mine, up_other = halves(w_up, 1)
    got = swap_core(jnp.stack([gate_other, up_other]))
    chip = [ordered(gate_mine, got[0], 0), ordered(up_mine, got[1], 0)]
    pieces = []
    for chunk in chip:
        column = jnp.concatenate([chunk] + [shift_z(chunk, -step) for step in (1, 2, 3)], 0).T
        pieces.append([column] + [shift_x(column, -step) for step in (1, 2, 3)])

    inputs_t = jnp.concatenate([inputs, swap_core(inputs)], 0).T
    upstream_mine, upstream_other = halves(upstream.T, 0)
    upstream_pair = jnp.concatenate([upstream_mine, swap_core(upstream_other)], 1)
    gain_wide = jnp.broadcast_to(gain[:, None], (width, tokens))
    normed, root_mean = call(
        norm_kernel,
        (shape((width, 2 * tokens), BF), shape((1, 2 * tokens), F32)),
        [SMEM, VMEM, VMEM],
    )(spot, inputs_t, gain_wide)

    hidden_pair, back, part_own, part_other = call(
        forward_kernel,
        (
            shape((half, 2 * tokens), BF),
            shape((2, half, 2 * tokens), BF),
            shape((width, tokens), F32),
            shape((width, tokens), BF),
        ),
        [VMEM] * (2 + 2 * NX),
    )(normed, upstream_pair, *pieces[0], *pieces[1])
    part_other = swap_core(part_other)
    terms = call(
        gradient_kernel,
        tuple(shape((2, half, column_rows), F32 if index == 0 else BF) for index in range(NX)),
        [VMEM] * 2,
    )(normed, back)
    travelling = [shift_x(terms[steps], steps) for steps in (2, 1, 3)]
    hidden_other = swap_core(hidden_pair[:, tokens:])
    hidden = ordered(hidden_pair[:, :tokens], hidden_other, 0).T

    spare = 16
    sending = call(
        blocks_kernel, shape((n_dp, features + spare, tokens), BF), [SMEM] + [VMEM] * 5
    )(spot, part_own, part_other, inputs_t[:, :tokens], root_mean[:, :tokens], gain_wide)
    got = lax.all_to_all(sending, "dp", 0, 0, tiled=True)
    totals = jnp.sum(got.astype(F32), axis=0)
    own_sums = totals[:features]
    token_totals = totals[features] + totals[features + 1] + totals[features + 2]
    start = lax.axis_index("dp") * features
    gain_slice = lax.dynamic_slice_in_dim(gain, start, features, 0)[:, None]
    root_own = root_mean[:, :tokens]
    unit_slice = (
        lax.dynamic_slice_in_dim(inputs_t[:, :tokens], start, features, 0).astype(F32) / root_own
    )
    grad_input = (
        ((own_sums * gain_slice - unit_slice * (token_totals / width)[None, :]) / root_own)
        .astype(BF)
        .T
    )
    gain_part = jnp.sum(own_sums * unit_slice, axis=1)
    gain_part = lax.psum(gain_part, "blk", axis_index_groups=X_GROUPS)
    gain_part = lax.psum(gain_part, "blk", axis_index_groups=Z_GROUPS)
    grad_gain = gain_part + swap_core(gain_part)

    column_sum = terms[0]
    for value in travelling:
        column_sum = column_sum + value.astype(F32)
    column_sum = column_sum.reshape(columns, column_rows).T.reshape(NZ, rows * NC, columns)
    chip_sum = column_sum[0]
    for step in (2, 1, 3):
        chip_sum = chip_sum + shift_z(column_sum[step].astype(BF), step).astype(F32)
    sum_mine, sum_other = chip_sum[:rows], chip_sum[rows:]
    sum_mine, sum_other = (
        jnp.where(first, sum_mine, sum_other),
        jnp.where(first, sum_other, sum_mine),
    )
    sum_other = swap_core(sum_other)
    grad_gate = ordered(sum_mine[:, :half], sum_other[:, :half], 1)
    grad_up = ordered(sum_mine[:, half:], sum_other[:, half:], 1)
    return (hidden, grad_gate, grad_up, grad_input, grad_gain)


def solution(mesh):
    return jax.shard_map(
        per_device,
        mesh=mesh,
        in_specs=(P("blk", None), P(), P("blk", "dp"), P("blk", "dp"), P("blk", "dp")),
        out_specs=(P("blk", "dp"), P("blk", "dp"), P("blk", "dp"), P("blk", "dp"), P("dp")),
        check_vma=False,
    )
```

```python
import jax
import jax.numpy as jnp
from jax import lax
from jax.experimental import pallas as pl
from jax.experimental.pallas import tpu as pltpu
from jax.sharding import PartitionSpec as P

BF = jnp.bfloat16
F32 = jnp.float32
NX, NZ, NC = 4, 4, 2
VMEM = pl.BlockSpec(memory_space=pltpu.VMEM)
SMEM = pl.BlockSpec(memory_space=pltpu.SMEM)
PARAMS = pltpu.CompilerParams(vmem_limit_bytes=48 * 1024 * 1024)
NT = (((1,), (1,)), ((), ()))
TN = (((0,), (0,)), ((), ()))


def place(x, z, c):
    return (x * NZ + z) * NC + c


def pairs(move):
    return [
        (place(x, z, c), place(*move(x, z, c)))
        for x in range(NX)
        for z in range(NZ)
        for c in range(NC)
    ]


def swap_core(value):
    return lax.ppermute(value, "blk", pairs(lambda x, z, c: (x, z, 1 - c)))


def shift_x(value, steps):
    return lax.ppermute(value, "blk", pairs(lambda x, z, c: ((x + steps) % NX, z, c)))


NH = 2


def y_groups(count):
    return [[index * NH + high for index in range(count // NH)] for high in range(NH)]


X_GROUPS = [[place(x, z, c) for x in range(NX)] for z in range(NZ) for c in range(NC)]
Z_GROUPS = [[place(x, z, c) for z in range(NZ)] for x in range(NX) for c in range(NC)]


def norm_kernel(x_ref, gain_ref, normed_ref, root_ref):
    width, tokens = x_ref.shape
    size = width // (NX * NZ)
    total = jnp.zeros((size, tokens), F32)
    for index in range(NX * NZ):
        value = x_ref[pl.ds(index * size, size), :].astype(F32)
        total += value * value
    root = jnp.sqrt(jnp.sum(total, axis=0, keepdims=True) / width + 1e-05)
    root_ref[...] = root
    for index in range(NX * NZ):
        rows = pl.ds(index * size, size)
        unit = x_ref[rows, :].astype(F32) / root
        gain = gain_ref[rows, :]
        gain = jnp.concatenate([gain, gain], axis=1)
        normed_ref[rows, :] = (unit * gain).astype(BF)


def forward_kernel(
    normed_ref, upstream_ref, weight_ref, hidden_ref, back_ref, own_ref, other_ref
):
    size = weight_ref.shape[3]
    tokens = own_ref.shape[1]

    def product(which):
        total = None
        for index in range(NX):
            term = jnp.dot(
                weight_ref[index, which],
                normed_ref[pl.ds(index * size, size), :],
                preferred_element_type=F32,
            )
            total = term if total is None else total + term
        return total

    gate_pre = product(0)
    up_pre = product(1)
    sigmoid = 1.0 / (1.0 + jnp.exp(-gate_pre))
    activated = gate_pre * sigmoid
    hidden_ref[...] = (activated * up_pre).astype(BF)
    upstream = upstream_ref[...].astype(F32)
    back_up = (upstream * activated).astype(BF)
    back_gate = (upstream * up_pre * sigmoid * (1.0 + gate_pre * (1.0 - sigmoid))).astype(BF)
    back_ref[0] = back_gate
    back_ref[1] = back_up
    for index in range(NX):
        part = lax.dot_general(weight_ref[index, 0], back_gate, TN, preferred_element_type=F32)
        part += lax.dot_general(weight_ref[index, 1], back_up, TN, preferred_element_type=F32)
        rows = pl.ds(index * size, size)
        own_ref[rows, :] = part[:, :tokens]
        other_ref[rows, :] = part[:, tokens:].astype(BF)


def gradient_kernel(spot_ref, normed_ref, back_ref, *outs):
    size = outs[0].shape[2]
    for index in range(NX):
        block = (spot_ref[0] + index) % NX
        rows = normed_ref[pl.ds(pl.multiple_of(block * size, size), size), :]
        for which in range(2):
            term = lax.dot_general(back_ref[which], rows, NT, preferred_element_type=F32)
            outs[index][which] = term.astype(outs[index].dtype)


def blocks_kernel(own_ref, other_ref, x_ref, root_ref, gain_ref, out_ref):
    width, tokens = own_ref.shape
    size = width // (NX * NZ)
    root = root_ref[...]
    total = jnp.zeros((size, tokens), F32)
    for index in range(NX * NZ):
        rows = pl.ds(index * size, size)
        part = (own_ref[rows, :] + other_ref[rows, :].astype(F32)).astype(BF)
        out_ref[index, 0:size, :] = part
        unit = x_ref[rows, :].astype(F32) / root
        total += part.astype(F32) * gain_ref[rows, :] * unit
    dots = jnp.sum(total, axis=0, keepdims=True)
    high = dots.astype(BF).astype(F32)
    mid = (dots - high).astype(BF).astype(F32)
    low = dots - high - mid
    spare = out_ref.shape[1] - size
    line = lax.broadcasted_iota(jnp.int32, (spare, tokens), 0)
    rows = jnp.where(line == 0, high, jnp.where(line == 1, mid, jnp.where(line == 2, low, 0.0)))
    for index in range(NX * NZ):
        out_ref[index, size : size + spare, :] = rows.astype(BF)


def call(kernel, outs, specs):
    return pl.pallas_call(
        kernel,
        out_shape=outs,
        in_specs=specs,
        out_specs=jax.tree.map(lambda _: VMEM, outs),
        compiler_params=PARAMS,
    )


def shape(dims, dtype):
    return jax.ShapeDtypeStruct(dims, dtype)


def per_device(inputs, gain, w_gate, w_up, upstream):
    position = lax.axis_index("blk")
    core = position % NC
    spot = (position // (NZ * NC)).astype(jnp.int32).reshape(1)
    first = core == 0
    tokens, width = inputs.shape
    rows, columns = w_gate.shape
    half = columns // 2
    n_dp = lax.axis_size("dp")
    features = width // n_dp
    column_rows = rows * NZ * NC

    def ordered(own, other, axis):
        return jnp.where(
            first, jnp.concatenate([own, other], axis), jnp.concatenate([other, own], axis)
        )

    def halves(value, axis):
        low, high = jnp.split(value, 2, axis)
        return jnp.where(first, low, high), jnp.where(first, high, low)

    gate_mine, gate_other = halves(w_gate, 1)
    up_mine, up_other = halves(w_up, 1)
    weight_other = swap_core(jnp.concatenate([gate_other, up_other], 1))
    chip = ordered(jnp.concatenate([gate_mine, up_mine], 1), weight_other, 0)
    column = lax.all_gather(chip, "blk", axis=0, tiled=True, axis_index_groups=Z_GROUPS).T
    copies = jnp.broadcast_to(column.reshape(2, half, column_rows), (NX, 2, half, column_rows))
    weight = lax.all_to_all(copies, "blk", 0, 0, tiled=True, axis_index_groups=X_GROUPS)

    inputs_t = jnp.concatenate([inputs, swap_core(inputs)], 0).T
    upstream_mine, upstream_other = halves(upstream.T, 0)
    upstream_pair = jnp.concatenate([upstream_mine, swap_core(upstream_other)], 1)
    gain_wide = jnp.broadcast_to(gain[:, None], (width, tokens))
    normed, root_mean = call(
        norm_kernel,
        (shape((width, 2 * tokens), BF), shape((1, 2 * tokens), F32)),
        [VMEM] * 2,
    )(inputs_t, gain_wide)

    hidden_pair, back, part_own, part_other = call(
        forward_kernel,
        (
            shape((half, 2 * tokens), BF),
            shape((2, half, 2 * tokens), BF),
            shape((width, tokens), F32),
            shape((width, tokens), BF),
        ),
        [VMEM] * 3,
    )(normed, upstream_pair, weight)
    part_other = swap_core(part_other)
    terms = call(
        gradient_kernel,
        tuple(shape((2, half, column_rows), F32 if index == 0 else BF) for index in range(NX)),
        [SMEM] + [VMEM] * 2,
    )(spot, normed, back)
    travelling = [shift_x(terms[steps], steps) for steps in (2, 1, 3)]
    hidden_other = swap_core(hidden_pair[:, tokens:])
    hidden = ordered(hidden_pair[:, :tokens], hidden_other, 0).T

    spare = 16
    sending = call(blocks_kernel, shape((n_dp, features + spare, tokens), BF), [VMEM] * 5)(
        part_own, part_other, inputs_t[:, :tokens], root_mean[:, :tokens], gain_wide
    )
    sending = sending.reshape(n_dp // NH, NH * (features + spare), tokens)
    got = lax.all_to_all(sending, "dp", 0, 0, tiled=True, axis_index_groups=y_groups(n_dp))
    got, travelling = lax.optimization_barrier((got, travelling))
    y_sums = jnp.sum(got.astype(F32), axis=0).reshape(NH, features + spare, tokens)
    low_half = lax.axis_index("dp") % NH == 0
    totals = jnp.where(low_half, y_sums[0], y_sums[1]) + lax.ppermute(
        jnp.where(low_half, y_sums[1], y_sums[0]),
        "dp",
        [(index, index ^ 1) for index in range(n_dp)],
    )
    own_sums = totals[:features]
    token_totals = totals[features] + totals[features + 1] + totals[features + 2]
    start = lax.axis_index("dp") * features
    gain_slice = lax.dynamic_slice_in_dim(gain, start, features, 0)[:, None]
    root_own = root_mean[:, :tokens]
    unit_slice = (
        lax.dynamic_slice_in_dim(inputs_t[:, :tokens], start, features, 0).astype(F32) / root_own
    )
    grad_input = (
        ((own_sums * gain_slice - unit_slice * (token_totals / width)[None, :]) / root_own)
        .astype(BF)
        .T
    )
    gain_part = jnp.sum(own_sums * unit_slice, axis=1)
    gain_part = lax.psum(gain_part, "blk", axis_index_groups=X_GROUPS)
    gain_part = lax.psum(gain_part, "blk", axis_index_groups=Z_GROUPS)

    column_sum = terms[0]
    for value in travelling:
        column_sum = column_sum + value.astype(F32)
    column_sum = column_sum.reshape(columns, column_rows).T.astype(BF)
    blocks = lax.all_to_all(
        column_sum.reshape(NZ, rows * NC, columns),
        "blk",
        0,
        0,
        tiled=True,
        axis_index_groups=Z_GROUPS,
    )
    chip_sum = jnp.sum(blocks.astype(F32), axis=0)
    sum_mine, sum_other = chip_sum[:rows], chip_sum[rows:]
    sum_mine, sum_other = (
        jnp.where(first, sum_mine, sum_other),
        jnp.where(first, sum_other, sum_mine),
    )
    gain_row = jnp.pad(gain_part, (0, columns - features))[None, :]
    other = swap_core(jnp.concatenate([sum_other, gain_row], 0))
    sum_other = other[:rows]
    grad_gain = gain_part + other[rows, :features]
    grad_gate = ordered(sum_mine[:, :half], sum_other[:, :half], 1)
    grad_up = ordered(sum_mine[:, half:], sum_other[:, half:], 1)
    return (hidden, grad_gate, grad_up, grad_input, grad_gain)


def solution(mesh):
    return jax.shard_map(
        per_device,
        mesh=mesh,
        in_specs=(P("blk", None), P(), P("blk", "dp"), P("blk", "dp"), P("blk", "dp")),
        out_specs=(P("blk", "dp"), P("blk", "dp"), P("blk", "dp"), P("blk", "dp"), P("dp")),
        check_vma=False,
    )
```

```python
import jax
import jax.numpy as jnp
from jax import lax
from jax.experimental import pallas as pl
from jax.experimental.pallas import tpu as pltpu
from jax.sharding import PartitionSpec as P

BF = jnp.bfloat16
F32 = jnp.float32
NX, NZ, NC, NH = 4, 4, 2, 2
VMEM = pl.BlockSpec(memory_space=pltpu.VMEM)
SMEM = pl.BlockSpec(memory_space=pltpu.SMEM)
PARAMS = pltpu.CompilerParams(vmem_limit_bytes=48 * 1024 * 1024)
NT = (((1,), (1,)), ((), ()))
TN = (((0,), (0,)), ((), ()))


def swap(value, axis):
    return lax.ppermute(value, axis, [(0, 1), (1, 0)])


def swap_core(value):
    return swap(value, "c")


def shift_x(value, steps):
    return lax.ppermute(value, "x", [(x, (x + steps) % NX) for x in range(NX)])


def norm_kernel(x_ref, gain_ref, normed_ref, root_ref):
    width, tokens = x_ref.shape
    size = width // (NX * NZ)
    total = jnp.zeros((size, tokens), F32)
    for index in range(NX * NZ):
        value = x_ref[pl.ds(index * size, size), :].astype(F32)
        total += value * value
    root = jnp.sqrt(jnp.sum(total, axis=0, keepdims=True) / width + 1e-05)
    root_ref[...] = root
    for index in range(NX * NZ):
        rows = pl.ds(index * size, size)
        unit = x_ref[rows, :].astype(F32) / root
        gain = gain_ref[rows, :]
        gain = jnp.concatenate([gain, gain], axis=1)
        normed_ref[rows, :] = (unit * gain).astype(BF)


def forward_kernel(
    normed_ref, upstream_ref, weight_ref, hidden_ref, back_ref, own_ref, other_ref
):
    size = weight_ref.shape[3]
    tokens = own_ref.shape[1]

    def product(which):
        total = None
        for index in range(NX):
            term = jnp.dot(
                weight_ref[index, which],
                normed_ref[pl.ds(index * size, size), :],
                preferred_element_type=F32,
            )
            total = term if total is None else total + term
        return total

    gate_pre = product(0)
    up_pre = product(1)
    sigmoid = 1.0 / (1.0 + jnp.exp(-gate_pre))
    activated = gate_pre * sigmoid
    hidden_ref[...] = (activated * up_pre).astype(BF)
    upstream = upstream_ref[...].astype(F32)
    back_up = (upstream * activated).astype(BF)
    back_gate = (upstream * up_pre * sigmoid * (1.0 + gate_pre * (1.0 - sigmoid))).astype(BF)
    back_ref[0] = back_gate
    back_ref[1] = back_up
    for index in range(NX):
        part = lax.dot_general(weight_ref[index, 0], back_gate, TN, preferred_element_type=F32)
        part += lax.dot_general(weight_ref[index, 1], back_up, TN, preferred_element_type=F32)
        rows = pl.ds(index * size, size)
        own_ref[rows, :] = part[:, :tokens]
        other_ref[rows, :] = part[:, tokens:].astype(BF)


def gradient_kernel(spot_ref, normed_ref, back_ref, *outs):
    size = outs[0].shape[2]
    for index in range(NX):
        block = (spot_ref[0] + index) % NX
        rows = normed_ref[pl.ds(pl.multiple_of(block * size, size), size), :]
        for which in range(2):
            term = lax.dot_general(back_ref[which], rows, NT, preferred_element_type=F32)
            outs[index][which] = term.astype(outs[index].dtype)


def blocks_kernel(own_ref, other_ref, x_ref, root_ref, gain_ref, out_ref):
    width, tokens = own_ref.shape
    size = width // (NX * NZ)
    root = root_ref[...]
    total = jnp.zeros((size, tokens), F32)
    for index in range(NX * NZ):
        rows = pl.ds(index * size, size)
        part = (own_ref[rows, :] + other_ref[rows, :].astype(F32)).astype(BF)
        out_ref[index, 0:size, :] = part
        unit = x_ref[rows, :].astype(F32) / root
        total += part.astype(F32) * gain_ref[rows, :] * unit
    dots = jnp.sum(total, axis=0, keepdims=True)
    high = dots.astype(BF).astype(F32)
    mid = (dots - high).astype(BF).astype(F32)
    low = dots - high - mid
    spare = out_ref.shape[1] - size
    line = lax.broadcasted_iota(jnp.int32, (spare, tokens), 0)
    rows = jnp.where(line == 0, high, jnp.where(line == 1, mid, jnp.where(line == 2, low, 0.0)))
    for index in range(NX * NZ):
        out_ref[index, size : size + spare, :] = rows.astype(BF)


def call(kernel, outs, specs):
    return pl.pallas_call(
        kernel,
        out_shape=outs,
        in_specs=specs,
        out_specs=jax.tree.map(lambda _: VMEM, outs),
        compiler_params=PARAMS,
    )


def shape(dims, dtype):
    return jax.ShapeDtypeStruct(dims, dtype)


def per_device(inputs, gain, w_gate, w_up, upstream):
    spot = lax.axis_index("x").astype(jnp.int32).reshape(1)
    first = lax.axis_index("c") == 0
    tokens, width = inputs.shape
    rows, columns = w_gate.shape
    half = columns // 2
    n_dp = lax.axis_size(("y", "h"))
    features = width // n_dp
    column_rows = rows * NZ * NC

    def ordered(own, other, axis):
        return jnp.where(
            first, jnp.concatenate([own, other], axis), jnp.concatenate([other, own], axis)
        )

    def halves(value, axis):
        low, high = jnp.split(value, 2, axis)
        return jnp.where(first, low, high), jnp.where(first, high, low)

    gate_mine, gate_other = halves(w_gate, 1)
    up_mine, up_other = halves(w_up, 1)
    weight_other = swap_core(jnp.concatenate([gate_other, up_other], 1))
    chip = ordered(jnp.concatenate([gate_mine, up_mine], 1), weight_other, 0)
    column = lax.all_gather(chip, "z", axis=0, tiled=True).T
    copies = jnp.broadcast_to(column.reshape(2, half, column_rows), (NX, 2, half, column_rows))
    weight = lax.all_to_all(copies, "x", 0, 0, tiled=True)

    inputs_t = jnp.concatenate([inputs, swap_core(inputs)], 0).T
    upstream_mine, upstream_other = halves(upstream.T, 0)
    upstream_pair = jnp.concatenate([upstream_mine, swap_core(upstream_other)], 1)
    gain_wide = jnp.broadcast_to(gain[:, None], (width, tokens))
    normed, root_mean = call(
        norm_kernel,
        (shape((width, 2 * tokens), BF), shape((1, 2 * tokens), F32)),
        [VMEM] * 2,
    )(inputs_t, gain_wide)

    hidden_pair, back, part_own, part_other = call(
        forward_kernel,
        (
            shape((half, 2 * tokens), BF),
            shape((2, half, 2 * tokens), BF),
            shape((width, tokens), F32),
            shape((width, tokens), BF),
        ),
        [VMEM] * 3,
    )(normed, upstream_pair, weight)
    part_other = swap_core(part_other)
    terms = call(
        gradient_kernel,
        tuple(shape((2, half, column_rows), F32 if index == 0 else BF) for index in range(NX)),
        [SMEM] + [VMEM] * 2,
    )(spot, normed, back)
    travelling = [shift_x(terms[steps], steps) for steps in (2, 1, 3)]
    hidden_other = swap_core(hidden_pair[:, tokens:])
    hidden = ordered(hidden_pair[:, :tokens], hidden_other, 0).T

    spare = 16
    sending = call(blocks_kernel, shape((n_dp, features + spare, tokens), BF), [VMEM] * 5)(
        part_own, part_other, inputs_t[:, :tokens], root_mean[:, :tokens], gain_wide
    )
    sending = sending.reshape(n_dp // NH, NH * (features + spare), tokens)
    got = lax.all_to_all(sending, "y", 0, 0, tiled=True)
    y_sums = jnp.sum(got.astype(F32), axis=0).reshape(NH, features + spare, tokens)
    low_half = lax.axis_index("h") == 0
    totals = jnp.where(low_half, y_sums[0], y_sums[1]) + swap(
        jnp.where(low_half, y_sums[1], y_sums[0]), "h"
    )
    own_sums = totals[:features]
    token_totals = totals[features] + totals[features + 1] + totals[features + 2]
    start = lax.axis_index(("y", "h")) * features
    gain_slice = lax.dynamic_slice_in_dim(gain, start, features, 0)[:, None]
    root_own = root_mean[:, :tokens]
    unit_slice = (
        lax.dynamic_slice_in_dim(inputs_t[:, :tokens], start, features, 0).astype(F32) / root_own
    )
    grad_input = (
        ((own_sums * gain_slice - unit_slice * (token_totals / width)[None, :]) / root_own)
        .astype(BF)
        .T
    )
    gain_part = jnp.sum(own_sums * unit_slice, axis=1)
    grad_input, gain_part, travelling = lax.optimization_barrier(
        (grad_input, gain_part, travelling)
    )
    grad_gain = lax.psum(lax.psum(gain_part, "x"), "z")
    grad_gain = grad_gain + swap_core(grad_gain)

    column_sum = terms[0]
    for value in travelling:
        column_sum = column_sum + value.astype(F32)
    column_sum = column_sum.reshape(columns, column_rows).T.astype(BF)
    blocks = lax.all_to_all(
        column_sum.reshape(NZ * NC, rows, columns), ("z", "c"), 0, 0, tiled=True
    )
    sums = jnp.sum(blocks.reshape(NZ, NC, rows, columns).astype(F32), axis=0)
    grad_gate = jnp.concatenate([sums[0, :, :half], sums[1, :, :half]], 1)
    grad_up = jnp.concatenate([sums[0, :, half:], sums[1, :, half:]], 1)
    return (hidden, grad_gate, grad_up, grad_input, grad_gain)


def solution(mesh):
    fine = jax.sharding.Mesh(mesh.devices.reshape(NX, NZ, NC, -1, NH), ("x", "z", "c", "y", "h"))
    blk, dp = ("x", "z", "c"), ("y", "h")
    return jax.shard_map(
        per_device,
        mesh=fine,
        in_specs=(P(blk, None), P(), P(blk, dp), P(blk, dp), P(blk, dp)),
        out_specs=(P(blk, dp), P(blk, dp), P(blk, dp), P(blk, dp), P(dp)),
        check_vma=False,
    )
```

```python
import jax
import jax.numpy as jnp
from jax import lax
from jax.experimental import pallas as pl
from jax.experimental.pallas import tpu as pltpu
from jax.sharding import PartitionSpec as P

BF = jnp.bfloat16
F32 = jnp.float32
NX, NZ, NC, NH = 4, 4, 2, 2
VMEM = pl.BlockSpec(memory_space=pltpu.VMEM)
SMEM = pl.BlockSpec(memory_space=pltpu.SMEM)
PARAMS = pltpu.CompilerParams(vmem_limit_bytes=48 * 1024 * 1024)
NT = (((1,), (1,)), ((), ()))
TN = (((0,), (0,)), ((), ()))


def swap(value, axis):
    return lax.ppermute(value, axis, [(0, 1), (1, 0)])


def swap_core(value):
    return swap(value, "c")


def shift_x(value, steps):
    return lax.ppermute(value, "x", [(x, (x + steps) % NX) for x in range(NX)])


def moved(block, core):
    return (block // NZ * NC + core) * NZ + block % NZ


def norm_kernel(x_ref, gain_ref, normed_ref, root_ref):
    width, tokens = x_ref.shape
    size = width // (NX * NZ)
    total = jnp.zeros((size, tokens), F32)
    for index in range(NX * NZ):
        value = x_ref[pl.ds(index * size, size), :].astype(F32)
        total += value * value
    root = jnp.sqrt(jnp.sum(total, axis=0, keepdims=True) / width + 1e-05)
    root_ref[...] = root
    for index in range(NX * NZ):
        rows = pl.ds(index * size, size)
        unit = x_ref[rows, :].astype(F32) / root
        gain = gain_ref[rows, :]
        value = (unit * jnp.concatenate([gain, gain], axis=1)).astype(BF)
        for core in range(NC):
            chunk = size // NC
            normed_ref[pl.ds(moved(index, core) * chunk, chunk), :] = value[
                core * chunk : (core + 1) * chunk
            ]


def forward_kernel(
    normed_ref, upstream_ref, weight_ref, hidden_ref, back_ref, own_ref, other_ref
):
    size = weight_ref.shape[2] // 2
    tokens = own_ref.shape[1]

    def piece(index, which):
        return weight_ref[index, :, which * size : (which + 1) * size]

    def product(which):
        total = None
        for index in range(NX * NC):
            term = jnp.dot(
                piece(index, which),
                normed_ref[pl.ds(index * size, size), :],
                preferred_element_type=F32,
            )
            total = term if total is None else total + term
        return total

    gate_pre = product(0)
    up_pre = product(1)
    sigmoid = 1.0 / (1.0 + jnp.exp(-gate_pre))
    activated = gate_pre * sigmoid
    hidden_ref[...] = (activated * up_pre).astype(BF)
    upstream = upstream_ref[...].astype(F32)
    back_up = (upstream * activated).astype(BF)
    back_gate = (upstream * up_pre * sigmoid * (1.0 + gate_pre * (1.0 - sigmoid))).astype(BF)
    back_ref[0] = back_gate
    back_ref[1] = back_up
    for index in range(NX * NC):
        part = lax.dot_general(piece(index, 0), back_gate, TN, preferred_element_type=F32)
        part += lax.dot_general(piece(index, 1), back_up, TN, preferred_element_type=F32)
        rows = pl.ds(index * size, size)
        own_ref[rows, :] = part[:, :tokens]
        other_ref[rows, :] = part[:, tokens:].astype(BF)


def gradient_kernel(spot_ref, normed_ref, back_ref, *outs):
    size = outs[0].shape[2]
    for index in range(NX):
        block = (spot_ref[0] + index) % NX
        rows = normed_ref[pl.ds(pl.multiple_of(block * size, size), size), :]
        for which in range(2):
            term = lax.dot_general(back_ref[which], rows, NT, preferred_element_type=F32)
            outs[index][which] = term.astype(outs[index].dtype)


def blocks_kernel(own_ref, other_ref, x_ref, root_ref, gain_ref, out_ref):
    width, tokens = own_ref.shape
    size = width // (NX * NZ)
    root = root_ref[...]
    total = jnp.zeros((size, tokens), F32)
    for index in range(NX * NZ):
        rows = pl.ds(index * size, size)
        chunk = size // NC
        places = [pl.ds(moved(index, core) * chunk, chunk) for core in range(NC)]
        own = jnp.concatenate([own_ref[here, :] for here in places], axis=0)
        other = jnp.concatenate([other_ref[here, :] for here in places], axis=0)
        part = (own + other.astype(F32)).astype(BF)
        out_ref[index, 0:size, :] = part
        unit = x_ref[rows, :].astype(F32) / root
        total += part.astype(F32) * gain_ref[rows, :] * unit
    dots = jnp.sum(total, axis=0, keepdims=True)
    high = dots.astype(BF).astype(F32)
    mid = (dots - high).astype(BF).astype(F32)
    low = dots - high - mid
    spare = out_ref.shape[1] - size
    line = lax.broadcasted_iota(jnp.int32, (spare, tokens), 0)
    rows = jnp.where(line == 0, high, jnp.where(line == 1, mid, jnp.where(line == 2, low, 0.0)))
    for index in range(NX * NZ):
        out_ref[index, size : size + spare, :] = rows.astype(BF)


def call(kernel, outs, specs):
    return pl.pallas_call(
        kernel,
        out_shape=outs,
        in_specs=specs,
        out_specs=jax.tree.map(lambda _: VMEM, outs),
        compiler_params=PARAMS,
    )


def shape(dims, dtype):
    return jax.ShapeDtypeStruct(dims, dtype)


def per_device(inputs, gain, w_gate, w_up, upstream):
    spot = lax.axis_index("x").astype(jnp.int32).reshape(1)
    first = lax.axis_index("c") == 0
    tokens, width = inputs.shape
    rows, columns = w_gate.shape
    half = columns // 2
    n_dp = lax.axis_size(("y", "h"))
    features = width // n_dp
    column_rows = rows * NZ * NC

    def ordered(own, other, axis):
        return jnp.where(
            first, jnp.concatenate([own, other], axis), jnp.concatenate([other, own], axis)
        )

    def halves(value, axis):
        low, high = jnp.split(value, 2, axis)
        return jnp.where(first, low, high), jnp.where(first, high, low)

    column = lax.all_gather(jnp.concatenate([w_gate, w_up], 1), "z", axis=0, tiled=True).T
    column = jnp.concatenate([column[:columns], column[columns:]], 1)
    copies = jnp.broadcast_to(
        column.reshape(NC, half, column_rows), (NX, NC, half, column_rows)
    ).reshape(NX * NC, half, column_rows)
    weight = lax.all_to_all(copies, ("x", "c"), 0, 0, tiled=True)

    inputs_t = jnp.concatenate([inputs, swap_core(inputs)], 0).T
    upstream_mine, upstream_other = halves(upstream.T, 0)
    upstream_pair = jnp.concatenate([upstream_mine, swap_core(upstream_other)], 1)
    gain_wide = jnp.broadcast_to(gain[:, None], (width, tokens))
    normed, root_mean = call(
        norm_kernel,
        (shape((width, 2 * tokens), BF), shape((1, 2 * tokens), F32)),
        [VMEM] * 2,
    )(inputs_t, gain_wide)

    hidden_pair, back, part_own, part_other = call(
        forward_kernel,
        (
            shape((half, 2 * tokens), BF),
            shape((2, half, 2 * tokens), BF),
            shape((width, tokens), F32),
            shape((width, tokens), BF),
        ),
        [VMEM] * 3,
    )(normed, upstream_pair, weight)
    part_other = swap_core(part_other)
    terms = call(
        gradient_kernel,
        tuple(shape((2, half, column_rows), F32 if index == 0 else BF) for index in range(NX)),
        [SMEM] + [VMEM] * 2,
    )(spot, normed, back)
    travelling = [shift_x(terms[steps], steps) for steps in (2, 1, 3)]
    hidden_other = swap_core(hidden_pair[:, tokens:])
    hidden = ordered(hidden_pair[:, :tokens], hidden_other, 0).T

    spare = 16
    sending = call(blocks_kernel, shape((n_dp, features + spare, tokens), BF), [VMEM] * 5)(
        part_own, part_other, inputs_t[:, :tokens], root_mean[:, :tokens], gain_wide
    )
    got = lax.all_to_all(sending, ("y", "h"), 0, 0, tiled=True)
    got, travelling = lax.optimization_barrier((got, travelling))
    totals = jnp.sum(got.astype(F32), axis=0)
    own_sums = totals[:features]
    token_totals = totals[features] + totals[features + 1] + totals[features + 2]
    start = lax.axis_index(("y", "h")) * features
    gain_slice = lax.dynamic_slice_in_dim(gain, start, features, 0)[:, None]
    root_own = root_mean[:, :tokens]
    unit_slice = (
        lax.dynamic_slice_in_dim(inputs_t[:, :tokens], start, features, 0).astype(F32) / root_own
    )
    grad_input = (
        ((own_sums * gain_slice - unit_slice * (token_totals / width)[None, :]) / root_own)
        .astype(BF)
        .T
    )
    gain_part = jnp.sum(own_sums * unit_slice, axis=1)
    grad_gain = lax.psum(lax.psum(gain_part, "x"), "z")
    grad_gain = grad_gain + swap_core(grad_gain)

    column_sum = terms[0]
    for value in travelling:
        column_sum = column_sum + value.astype(F32)
    column_sum = column_sum.reshape(columns, column_rows).T.astype(BF)
    blocks = lax.all_to_all(
        column_sum.reshape(NC * NZ, rows, columns), ("c", "z"), 0, 0, tiled=True
    )
    sums = jnp.sum(blocks.reshape(NC, NZ, rows, columns).astype(F32), axis=1)
    grad_gate = jnp.concatenate([sums[0, :, :half], sums[1, :, :half]], 1)
    grad_up = jnp.concatenate([sums[0, :, half:], sums[1, :, half:]], 1)
    return (hidden, grad_gate, grad_up, grad_input, grad_gain)


def solution(mesh):
    fine = jax.sharding.Mesh(mesh.devices.reshape(NX, NZ, NC, -1, NH), ("x", "z", "c", "y", "h"))
    blk, dp = ("x", "z", "c"), ("y", "h")
    return jax.shard_map(
        per_device,
        mesh=fine,
        in_specs=(P(blk, None), P(), P(blk, dp), P(blk, dp), P(blk, dp)),
        out_specs=(P(blk, dp), P(blk, dp), P(blk, dp), P(blk, dp), P(dp)),
        check_vma=False,
    )
```

```python
import jax
import jax.numpy as jnp
from jax import lax
from jax.experimental import pallas as pl
from jax.experimental.pallas import tpu as pltpu
from jax.sharding import PartitionSpec as P

BF = jnp.bfloat16
F32 = jnp.float32
NX, NZ, NC, NH = 4, 4, 2, 2
VMEM = pl.BlockSpec(memory_space=pltpu.VMEM)
SMEM = pl.BlockSpec(memory_space=pltpu.SMEM)
PARAMS = pltpu.CompilerParams(vmem_limit_bytes=48 * 1024 * 1024)
NT = (((1,), (1,)), ((), ()))
TN = (((0,), (0,)), ((), ()))


def swap(value, axis):
    return lax.ppermute(value, axis, [(0, 1), (1, 0)])


def swap_core(value):
    return swap(value, "c")


def shift_x(value, steps):
    return lax.ppermute(value, "x", [(x, (x + steps) % NX) for x in range(NX)])


def moved(block, core):
    return (block // NZ * NC + core) * NZ + block % NZ


def norm_kernel(x_ref, gain_ref, normed_ref, root_ref):
    width, tokens = x_ref.shape
    size = width // (NX * NZ)
    total = jnp.zeros((size, tokens), F32)
    for index in range(NX * NZ):
        value = x_ref[pl.ds(index * size, size), :].astype(F32)
        total += value * value
    root = jnp.sqrt(jnp.sum(total, axis=0, keepdims=True) / width + 1e-05)
    root_ref[...] = root
    for index in range(NX * NZ):
        rows = pl.ds(index * size, size)
        unit = x_ref[rows, :].astype(F32) / root
        gain = gain_ref[rows, :]
        value = (unit * jnp.concatenate([gain, gain], axis=1)).astype(BF)
        for core in range(NC):
            chunk = size // NC
            normed_ref[pl.ds(moved(index, core) * chunk, chunk), :] = value[
                core * chunk : (core + 1) * chunk
            ]


def forward_kernel(
    normed_ref, upstream_ref, weight_ref, hidden_ref, back_ref, own_ref, other_ref
):
    size = weight_ref.shape[2] // 2
    tokens = own_ref.shape[1]

    def piece(index, which):
        return weight_ref[index, :, which * size : (which + 1) * size]

    def product(which):
        total = None
        for index in range(NX * NC):
            term = jnp.dot(
                piece(index, which),
                normed_ref[pl.ds(index * size, size), :],
                preferred_element_type=F32,
            )
            total = term if total is None else total + term
        return total

    gate_pre = product(0)
    up_pre = product(1)
    sigmoid = 1.0 / (1.0 + jnp.exp(-gate_pre))
    activated = gate_pre * sigmoid
    hidden_ref[...] = (activated * up_pre).astype(BF)
    upstream = upstream_ref[...].astype(F32)
    back_up = (upstream * activated).astype(BF)
    back_gate = (upstream * up_pre * sigmoid * (1.0 + gate_pre * (1.0 - sigmoid))).astype(BF)
    back_ref[0] = back_gate
    back_ref[1] = back_up
    for index in range(NX * NC):
        part = lax.dot_general(piece(index, 0), back_gate, TN, preferred_element_type=F32)
        part += lax.dot_general(piece(index, 1), back_up, TN, preferred_element_type=F32)
        rows = pl.ds(index * size, size)
        own_ref[rows, :] = part[:, :tokens]
        other_ref[rows, :] = part[:, tokens:].astype(BF)


def gradient_kernel(spot_ref, normed_ref, back_ref, *outs):
    size = outs[0].shape[2]
    for index in range(NX):
        block = (spot_ref[0] + index) % NX
        rows = normed_ref[pl.ds(pl.multiple_of(block * size, size), size), :]
        for which in range(2):
            term = lax.dot_general(back_ref[which], rows, NT, preferred_element_type=F32)
            outs[index][which] = term.astype(outs[index].dtype)


def blocks_kernel(own_ref, other_ref, x_ref, root_ref, gain_ref, out_ref):
    width, tokens = own_ref.shape
    size = width // (NX * NZ)
    root = root_ref[...]
    total = jnp.zeros((size, tokens), F32)
    for index in range(NX * NZ):
        rows = pl.ds(index * size, size)
        chunk = size // NC
        places = [pl.ds(moved(index, core) * chunk, chunk) for core in range(NC)]
        own = jnp.concatenate([own_ref[here, :] for here in places], axis=0)
        other = jnp.concatenate([other_ref[here, :] for here in places], axis=0)
        part = (own + other.astype(F32)).astype(BF)
        out_ref[index, 0:size, :] = part
        unit = x_ref[rows, :].astype(F32) / root
        total += part.astype(F32) * gain_ref[rows, :] * unit
    dots = jnp.sum(total, axis=0, keepdims=True)
    high = dots.astype(BF).astype(F32)
    mid = (dots - high).astype(BF).astype(F32)
    low = dots - high - mid
    spare = out_ref.shape[1] - size
    line = lax.broadcasted_iota(jnp.int32, (spare, tokens), 0)
    rows = jnp.where(line == 0, high, jnp.where(line == 1, mid, jnp.where(line == 2, low, 0.0)))
    for index in range(NX * NZ):
        out_ref[index, size : size + spare, :] = rows.astype(BF)


def call(kernel, outs, specs):
    return pl.pallas_call(
        kernel,
        out_shape=outs,
        in_specs=specs,
        out_specs=jax.tree.map(lambda _: VMEM, outs),
        compiler_params=PARAMS,
    )


def shape(dims, dtype):
    return jax.ShapeDtypeStruct(dims, dtype)


def per_device(inputs, gain, w_gate, w_up, upstream):
    spot = lax.axis_index("x").astype(jnp.int32).reshape(1)
    first = lax.axis_index("c") == 0
    tokens, width = inputs.shape
    rows, columns = w_gate.shape
    half = columns // 2
    n_dp = lax.axis_size(("y", "h"))
    features = width // n_dp
    column_rows = rows * NZ * NC

    def ordered(own, other, axis):
        return jnp.where(
            first, jnp.concatenate([own, other], axis), jnp.concatenate([other, own], axis)
        )

    def halves(value, axis):
        low, high = jnp.split(value, 2, axis)
        return jnp.where(first, low, high), jnp.where(first, high, low)

    column = lax.all_gather(jnp.concatenate([w_gate, w_up], 1), "z", axis=0, tiled=True).T
    column = jnp.concatenate([column[:columns], column[columns:]], 1)
    copies = jnp.broadcast_to(
        column.reshape(NC, half, column_rows), (NX, NC, half, column_rows)
    ).reshape(NX * NC, half, column_rows)
    weight = lax.all_to_all(copies, ("x", "c"), 0, 0, tiled=True)

    inputs_t = jnp.concatenate([inputs, swap_core(inputs)], 0).T
    upstream_mine, upstream_other = halves(upstream.T, 0)
    upstream_pair = jnp.concatenate([upstream_mine, swap_core(upstream_other)], 1)
    gain_wide = jnp.broadcast_to(gain[:, None], (width, tokens))
    normed, root_mean = call(
        norm_kernel,
        (shape((width, 2 * tokens), BF), shape((1, 2 * tokens), F32)),
        [VMEM] * 2,
    )(inputs_t, gain_wide)

    hidden_pair, back, part_own, part_other = call(
        forward_kernel,
        (
            shape((half, 2 * tokens), BF),
            shape((2, half, 2 * tokens), BF),
            shape((width, tokens), F32),
            shape((width, tokens), BF),
        ),
        [VMEM] * 3,
    )(normed, upstream_pair, weight)
    part_other = swap_core(part_other)
    terms = call(
        gradient_kernel,
        tuple(shape((2, half, column_rows), F32 if index == 0 else BF) for index in range(NX)),
        [SMEM] + [VMEM] * 2,
    )(spot, normed, back)
    part_other, terms = lax.optimization_barrier((part_other, terms))
    travelling = [shift_x(terms[steps], steps) for steps in (2, 1, 3)]
    hidden_other = swap_core(hidden_pair[:, tokens:])

    spare = 16
    sending = call(blocks_kernel, shape((n_dp, features + spare, tokens), BF), [VMEM] * 5)(
        part_own, part_other, inputs_t[:, :tokens], root_mean[:, :tokens], gain_wide
    )
    got = lax.all_to_all(sending, ("y", "h"), 0, 0, tiled=True)
    got, travelling[0], hidden_other = lax.optimization_barrier(
        (got, travelling[0], hidden_other)
    )
    hidden = ordered(hidden_pair[:, :tokens], hidden_other, 0).T
    totals = jnp.sum(got.astype(F32), axis=0)
    own_sums = totals[:features]
    token_totals = totals[features] + totals[features + 1] + totals[features + 2]
    start = lax.axis_index(("y", "h")) * features
    gain_slice = lax.dynamic_slice_in_dim(gain, start, features, 0)[:, None]
    root_own = root_mean[:, :tokens]
    unit_slice = (
        lax.dynamic_slice_in_dim(inputs_t[:, :tokens], start, features, 0).astype(F32) / root_own
    )
    grad_input = (
        ((own_sums * gain_slice - unit_slice * (token_totals / width)[None, :]) / root_own)
        .astype(BF)
        .T
    )
    gain_part = jnp.sum(own_sums * unit_slice, axis=1)
    gain_part = lax.psum(gain_part, "x")
    gain_part, travelling = lax.optimization_barrier((gain_part, travelling))
    grad_gain = lax.psum(gain_part, "z")
    grad_gain = grad_gain + swap_core(grad_gain)

    column_sum = terms[0]
    for value in travelling:
        column_sum = column_sum + value.astype(F32)
    column_sum = column_sum.reshape(columns, column_rows).T.astype(BF)
    blocks = lax.all_to_all(
        column_sum.reshape(NC * NZ, rows, columns), ("c", "z"), 0, 0, tiled=True
    )
    sums = jnp.sum(blocks.reshape(NC, NZ, rows, columns).astype(F32), axis=1)
    grad_gate = jnp.concatenate([sums[0, :, :half], sums[1, :, :half]], 1)
    grad_up = jnp.concatenate([sums[0, :, half:], sums[1, :, half:]], 1)
    return (hidden, grad_gate, grad_up, grad_input, grad_gain)


def solution(mesh):
    fine = jax.sharding.Mesh(mesh.devices.reshape(NX, NZ, NC, -1, NH), ("x", "z", "c", "y", "h"))
    blk, dp = ("x", "z", "c"), ("y", "h")
    return jax.shard_map(
        per_device,
        mesh=fine,
        in_specs=(P(blk, None), P(), P(blk, dp), P(blk, dp), P(blk, dp)),
        out_specs=(P(blk, dp), P(blk, dp), P(blk, dp), P(blk, dp), P(dp)),
        check_vma=False,
    )
```

```python
import jax
import jax.numpy as jnp
from jax import lax
from jax.experimental import pallas as pl
from jax.experimental.pallas import tpu as pltpu
from jax.sharding import PartitionSpec as P

BF = jnp.bfloat16
F32 = jnp.float32
NX, NZ, NC, NH = 4, 4, 2, 2
ANY = pl.BlockSpec(memory_space=pl.ANY)
VMEM = pl.BlockSpec(memory_space=pltpu.VMEM)
PARAMS = pltpu.CompilerParams(vmem_limit_bytes=48 * 1024 * 1024)
NT = (((1,), (1,)), ((), ()))
TN = (((0,), (0,)), ((), ()))


def swap(value, axis):
    return lax.ppermute(value, axis, [(0, 1), (1, 0)])


def swap_core(value):
    return swap(value, "c")


def moved(block, core):
    return (block // NZ * NC + core) * NZ + block % NZ


def norm_kernel(x_ref, gain_ref, normed_ref, root_ref):
    width, tokens = x_ref.shape
    size = width // (NX * NZ)
    total = jnp.zeros((size, tokens), F32)
    for index in range(NX * NZ):
        value = x_ref[pl.ds(index * size, size), :].astype(F32)
        total += value * value
    root = jnp.sqrt(jnp.sum(total, axis=0, keepdims=True) / width + 1e-05)
    root_ref[...] = root
    for index in range(NX * NZ):
        rows = pl.ds(index * size, size)
        unit = x_ref[rows, :].astype(F32) / root
        gain = gain_ref[rows, :]
        value = (unit * jnp.concatenate([gain, gain], axis=1)).astype(BF)
        for core in range(NC):
            chunk = size // NC
            normed_ref[pl.ds(moved(index, core) * chunk, chunk), :] = value[
                core * chunk : (core + 1) * chunk
            ]


def forward_kernel(
    normed_ref, upstream_ref, weight_ref, hidden_ref, back_ref, own_ref, other_ref
):
    size = weight_ref.shape[2] // 2
    tokens = own_ref.shape[1]

    def piece(index, which):
        return weight_ref[index, :, which * size : (which + 1) * size]

    def product(which):
        total = None
        for index in range(NX * NC):
            term = jnp.dot(
                piece(index, which),
                normed_ref[pl.ds(index * size, size), :],
                preferred_element_type=F32,
            )
            total = term if total is None else total + term
        return total

    gate_pre = product(0)
    up_pre = product(1)
    sigmoid = 1.0 / (1.0 + jnp.exp(-gate_pre))
    activated = gate_pre * sigmoid
    hidden = activated * up_pre
    hidden_ref[...] = hidden[:, :tokens].astype(BF)
    width = own_ref.shape[0]
    extra = other_ref.shape[0] - width
    riding = jnp.concatenate(
        [hidden[:, tokens:], jnp.zeros((extra - hidden.shape[0], tokens), F32)], axis=0
    )
    other_ref[width : width + extra, :] = riding.astype(BF)
    upstream = upstream_ref[...].astype(F32)
    back_up = (upstream * activated).astype(BF)
    back_gate = (upstream * up_pre * sigmoid * (1.0 + gate_pre * (1.0 - sigmoid))).astype(BF)
    back_ref[0] = back_gate
    back_ref[1] = back_up
    for index in range(NX * NC):
        part = lax.dot_general(piece(index, 0), back_gate, TN, preferred_element_type=F32)
        part += lax.dot_general(piece(index, 1), back_up, TN, preferred_element_type=F32)
        rows = pl.ds(index * size, size)
        own_ref[rows, :] = part[:, :tokens]
        other_ref[rows, :] = part[:, tokens:].astype(BF)


def gradient_kernel(normed_ref, back_ref, out_ref):
    size = out_ref.shape[3]
    for index in range(NX):
        rows = normed_ref[pl.ds(index * size, size), :]
        for which in range(2):
            term = lax.dot_general(back_ref[which], rows, NT, preferred_element_type=F32)
            out_ref[index, which] = term.astype(BF)


def blocks_kernel(_, own_ref, other_ref, x_ref, root_ref, gain_ref, out_ref):
    width, tokens = own_ref.shape
    size = width // (NX * NZ)
    root = root_ref[...]
    total = jnp.zeros((size, tokens), F32)
    for index in range(NX * NZ):
        rows = pl.ds(index * size, size)
        chunk = size // NC
        places = [pl.ds(moved(index, core) * chunk, chunk) for core in range(NC)]
        own = jnp.concatenate([own_ref[here, :] for here in places], axis=0)
        other = jnp.concatenate([other_ref[here, :] for here in places], axis=0)
        part = (own + other.astype(F32)).astype(BF)
        out_ref[index, 0:size, :] = part
        unit = x_ref[rows, :].astype(F32) / root
        total += part.astype(F32) * gain_ref[rows, :] * unit
    dots = jnp.sum(total, axis=0, keepdims=True)
    high = dots.astype(BF).astype(F32)
    mid = (dots - high).astype(BF).astype(F32)
    low = dots - high - mid
    spare = out_ref.shape[1] - size
    line = lax.broadcasted_iota(jnp.int32, (spare, tokens), 0)
    rows = jnp.where(line == 0, high, jnp.where(line == 1, mid, jnp.where(line == 2, low, 0.0)))
    for index in range(NX * NZ):
        out_ref[index, size : size + spare, :] = rows.astype(BF)


def call(kernel, outs, specs):
    return pl.pallas_call(
        kernel,
        out_shape=outs,
        in_specs=specs,
        out_specs=jax.tree.map(lambda _: VMEM, outs),
        compiler_params=PARAMS,
    )


def shape(dims, dtype):
    return jax.ShapeDtypeStruct(dims, dtype)


def per_device(inputs, gain, w_gate, w_up, upstream):
    first = lax.axis_index("c") == 0
    tokens, width = inputs.shape
    rows, columns = w_gate.shape
    half = columns // 2
    n_dp = lax.axis_size(("y", "h"))
    features = width // n_dp
    column_rows = rows * NZ * NC

    def ordered(own, other, axis):
        return jnp.where(
            first, jnp.concatenate([own, other], axis), jnp.concatenate([other, own], axis)
        )

    def halves(value, axis):
        low, high = jnp.split(value, 2, axis)
        return jnp.where(first, low, high), jnp.where(first, high, low)

    column = lax.all_gather(jnp.concatenate([w_gate, w_up], 1), "z", axis=0, tiled=True).T
    column = jnp.concatenate([column[:columns], column[columns:]], 1)
    copies = jnp.broadcast_to(
        column.reshape(NC, half, column_rows), (NX, NC, half, column_rows)
    ).reshape(NX * NC, half, column_rows)
    weight = lax.all_to_all(copies, ("x", "c"), 0, 0, tiled=True)

    inputs_t = jnp.concatenate([inputs, swap_core(inputs)], 0).T
    upstream_mine, upstream_other = halves(upstream.T, 0)
    upstream_pair = jnp.concatenate([upstream_mine, swap_core(upstream_other)], 1)
    gain_wide = jnp.broadcast_to(gain[:, None], (width, tokens))
    normed, root_mean = call(
        norm_kernel,
        (shape((width, 2 * tokens), BF), shape((1, 2 * tokens), F32)),
        [VMEM] * 2,
    )(inputs_t, gain_wide)

    riding = -(-half // 16) * 16
    hidden_own, back, part_own, part_other = call(
        forward_kernel,
        (
            shape((half, tokens), BF),
            shape((2, half, 2 * tokens), BF),
            shape((width, tokens), F32),
            shape((width + riding, tokens), BF),
        ),
        [VMEM] * 3,
    )(normed, upstream_pair, weight)
    part_other = swap_core(part_other)
    hidden = ordered(hidden_own, part_other[width : width + half], 0).T
    terms = call(gradient_kernel, shape((NX, 2, half, column_rows), BF), [VMEM] * 2)(normed, back)

    spare = 16
    sending = call(blocks_kernel, shape((n_dp, features + spare, tokens), BF), [ANY] + [VMEM] * 5)(
        terms, part_own, part_other, inputs_t[:, :tokens], root_mean[:, :tokens], gain_wide
    )
    got = lax.all_to_all(sending, ("y", "h"), 0, 0, tiled=True)
    totals = jnp.sum(got.astype(F32), axis=0)
    own_sums = totals[:features]
    token_totals = totals[features] + totals[features + 1] + totals[features + 2]
    start = lax.axis_index(("y", "h")) * features
    gain_slice = lax.dynamic_slice_in_dim(gain, start, features, 0)[:, None]
    root_own = root_mean[:, :tokens]
    unit_slice = (
        lax.dynamic_slice_in_dim(inputs_t[:, :tokens], start, features, 0).astype(F32) / root_own
    )
    grad_input = (
        ((own_sums * gain_slice - unit_slice * (token_totals / width)[None, :]) / root_own)
        .astype(BF)
        .T
    )
    gain_part = jnp.sum(own_sums * unit_slice, axis=1)
    grad_gain = lax.psum(lax.psum(gain_part, "x"), "z")
    grad_gain = grad_gain + swap_core(grad_gain)

    arrived = lax.all_to_all(terms, "x", 0, 0, tiled=True)
    column_sum = jnp.sum(arrived.astype(F32), axis=0)
    column_sum = column_sum.reshape(columns, column_rows).T.astype(BF)
    blocks = lax.all_to_all(
        column_sum.reshape(NC * NZ, rows, columns), ("c", "z"), 0, 0, tiled=True
    )
    sums = jnp.sum(blocks.reshape(NC, NZ, rows, columns).astype(F32), axis=1)
    grad_gate = jnp.concatenate([sums[0, :, :half], sums[1, :, :half]], 1)
    grad_up = jnp.concatenate([sums[0, :, half:], sums[1, :, half:]], 1)
    return (hidden, grad_gate, grad_up, grad_input, grad_gain)


def solution(mesh):
    fine = jax.sharding.Mesh(mesh.devices.reshape(NX, NZ, NC, -1, NH), ("x", "z", "c", "y", "h"))
    blk, dp = ("x", "z", "c"), ("y", "h")
    return jax.shard_map(
        per_device,
        mesh=fine,
        in_specs=(P(blk, None), P(), P(blk, dp), P(blk, dp), P(blk, dp)),
        out_specs=(P(blk, dp), P(blk, dp), P(blk, dp), P(blk, dp), P(dp)),
        check_vma=False,
    )
```

```python
import jax
import jax.numpy as jnp
from jax import lax
from jax.experimental import pallas as pl
from jax.experimental.pallas import tpu as pltpu
from jax.sharding import PartitionSpec as P

BF = jnp.bfloat16
F32 = jnp.float32
NX, NZ, NC, NH = 4, 4, 2, 2
ANY = pl.BlockSpec(memory_space=pl.ANY)
VMEM = pl.BlockSpec(memory_space=pltpu.VMEM)
SMEM = pl.BlockSpec(memory_space=pltpu.SMEM)
PARAMS = pltpu.CompilerParams(vmem_limit_bytes=48 * 1024 * 1024)
NT = (((1,), (1,)), ((), ()))
TN = (((0,), (0,)), ((), ()))


def swap(value, axis):
    return lax.ppermute(value, axis, [(0, 1), (1, 0)])


def swap_core(value):
    return swap(value, "c")


def shift_x(value, steps):
    return lax.ppermute(value, "x", [(x, (x + steps) % NX) for x in range(NX)])


def moved(block, core):
    return (block // NZ * NC + core) * NZ + block % NZ


def norm_kernel(x_ref, gain_ref, normed_ref, root_ref):
    width, tokens = x_ref.shape
    size = width // (NX * NZ)
    total = jnp.zeros((size, tokens), F32)
    for index in range(NX * NZ):
        value = x_ref[pl.ds(index * size, size), :].astype(F32)
        total += value * value
    root = jnp.sqrt(jnp.sum(total, axis=0, keepdims=True) / width + 1e-05)
    root_ref[...] = root
    for index in range(NX * NZ):
        rows = pl.ds(index * size, size)
        unit = x_ref[rows, :].astype(F32) / root
        gain = gain_ref[rows, :]
        value = (unit * jnp.concatenate([gain, gain], axis=1)).astype(BF)
        for core in range(NC):
            chunk = size // NC
            normed_ref[pl.ds(moved(index, core) * chunk, chunk), :] = value[
                core * chunk : (core + 1) * chunk
            ]


def forward_kernel(
    normed_ref, upstream_ref, weight_ref, hidden_ref, back_ref, own_ref, other_ref, held, sems
):
    size = weight_ref.shape[2] // 2
    tokens = own_ref.shape[1]
    width = own_ref.shape[0]
    copies = [
        pltpu.make_async_copy(weight_ref.at[index], held.at[index], sems.at[index])
        for index in range(NX * NC)
    ]
    for copy in copies:
        copy.start()

    def piece(index, which):
        return held[index, :, which * size : (which + 1) * size]

    gate_pre, up_pre = 0.0, 0.0
    for index in range(NX * NC):
        copies[index].wait()
        rows = normed_ref[pl.ds(index * size, size), :]
        gate_pre += jnp.dot(piece(index, 0), rows, preferred_element_type=F32)
        up_pre += jnp.dot(piece(index, 1), rows, preferred_element_type=F32)
    sigmoid = 1.0 / (1.0 + jnp.exp(-gate_pre))
    activated = gate_pre * sigmoid
    hidden = activated * up_pre
    hidden_ref[...] = hidden[:, :tokens].astype(BF)
    extra = other_ref.shape[0] - width
    riding = jnp.concatenate(
        [hidden[:, tokens:], jnp.zeros((extra - hidden.shape[0], tokens), F32)], axis=0
    )
    other_ref[width : width + extra, :] = riding.astype(BF)
    upstream = upstream_ref[...].astype(F32)
    back_up = (upstream * activated).astype(BF)
    back_gate = (upstream * up_pre * sigmoid * (1.0 + gate_pre * (1.0 - sigmoid))).astype(BF)
    back_ref[0] = back_gate
    back_ref[1] = back_up
    for index in range(NX * NC):
        part = lax.dot_general(piece(index, 0), back_gate, TN, preferred_element_type=F32)
        part += lax.dot_general(piece(index, 1), back_up, TN, preferred_element_type=F32)
        rows = pl.ds(index * size, size)
        own_ref[rows, :] = part[:, :tokens]
        other_ref[rows, :] = part[:, tokens:].astype(BF)


def gradient_kernel(spot_ref, normed_ref, back_ref, *outs):
    size = outs[0].shape[2]
    for index in range(NX):
        block = (spot_ref[0] + index) % NX
        rows = normed_ref[pl.ds(pl.multiple_of(block * size, size), size), :]
        for which in range(2):
            term = lax.dot_general(back_ref[which], rows, NT, preferred_element_type=F32)
            outs[index][which] = term.astype(outs[index].dtype)


def blocks_kernel(own_ref, other_ref, x_ref, root_ref, gain_ref, out_ref):
    width, tokens = own_ref.shape
    size = width // (NX * NZ)
    root = root_ref[...]
    total = jnp.zeros((size, tokens), F32)
    for index in range(NX * NZ):
        rows = pl.ds(index * size, size)
        chunk = size // NC
        places = [pl.ds(moved(index, core) * chunk, chunk) for core in range(NC)]
        own = jnp.concatenate([own_ref[here, :] for here in places], axis=0)
        other = jnp.concatenate([other_ref[here, :] for here in places], axis=0)
        part = (own + other.astype(F32)).astype(BF)
        out_ref[index, 0:size, :] = part
        unit = x_ref[rows, :].astype(F32) / root
        total += part.astype(F32) * gain_ref[rows, :] * unit
    dots = jnp.sum(total, axis=0, keepdims=True)
    high = dots.astype(BF).astype(F32)
    mid = (dots - high).astype(BF).astype(F32)
    low = dots - high - mid
    spare = out_ref.shape[1] - size
    line = lax.broadcasted_iota(jnp.int32, (spare, tokens), 0)
    rows = jnp.where(line == 0, high, jnp.where(line == 1, mid, jnp.where(line == 2, low, 0.0)))
    for index in range(NX * NZ):
        out_ref[index, size : size + spare, :] = rows.astype(BF)


def column_kernel(own_ref, first_ref, second_ref, third_ref, out_ref):
    half = own_ref.shape[1]
    for which in range(2):
        total = own_ref[which] + first_ref[which].astype(F32)
        total += second_ref[which].astype(F32) + third_ref[which].astype(F32)
        out_ref[:, which * half : (which + 1) * half] = total.T.astype(BF)


def call(kernel, outs, specs, scratch=()):
    return pl.pallas_call(
        kernel,
        out_shape=outs,
        in_specs=specs,
        scratch_shapes=scratch,
        out_specs=jax.tree.map(lambda _: VMEM, outs),
        compiler_params=PARAMS,
    )


def shape(dims, dtype):
    return jax.ShapeDtypeStruct(dims, dtype)


def per_device(inputs, gain, w_gate, w_up, upstream):
    spot = lax.axis_index("x").astype(jnp.int32).reshape(1)
    first = lax.axis_index("c") == 0
    tokens, width = inputs.shape
    rows, columns = w_gate.shape
    half = columns // 2
    n_dp = lax.axis_size(("y", "h"))
    features = width // n_dp
    column_rows = rows * NZ * NC

    def ordered(own, other, axis):
        return jnp.where(
            first, jnp.concatenate([own, other], axis), jnp.concatenate([other, own], axis)
        )

    def halves(value, axis):
        low, high = jnp.split(value, 2, axis)
        return jnp.where(first, low, high), jnp.where(first, high, low)

    column = lax.all_gather(jnp.concatenate([w_gate, w_up], 1), "z", axis=0, tiled=True).T
    column = jnp.concatenate([column[:columns], column[columns:]], 1)
    copies = jnp.broadcast_to(
        column.reshape(NC, half, column_rows), (NX, NC, half, column_rows)
    ).reshape(NX * NC, half, column_rows)
    weight = lax.all_to_all(copies, ("x", "c"), 0, 0, tiled=True)

    inputs_t = jnp.concatenate([inputs, swap_core(inputs)], 0).T
    upstream_mine, upstream_other = halves(upstream.T, 0)
    upstream_pair = jnp.concatenate([upstream_mine, swap_core(upstream_other)], 1)
    gain_wide = jnp.broadcast_to(gain[:, None], (width, tokens))
    normed, root_mean = call(
        norm_kernel,
        (shape((width, 2 * tokens), BF), shape((1, 2 * tokens), F32)),
        [VMEM] * 2,
    )(inputs_t, gain_wide)

    riding = -(-half // 16) * 16
    hidden_own, back, part_own, part_other = call(
        forward_kernel,
        (
            shape((half, tokens), BF),
            shape((2, half, 2 * tokens), BF),
            shape((width, tokens), F32),
            shape((width + riding, tokens), BF),
        ),
        [VMEM, VMEM, ANY],
        [pltpu.VMEM(weight.shape, BF), pltpu.SemaphoreType.DMA((NX * NC,))],
    )(normed, upstream_pair, weight)
    part_other = swap_core(part_other)
    hidden = ordered(hidden_own, part_other[width : width + half], 0).T
    terms = call(
        gradient_kernel,
        tuple(shape((2, half, column_rows), F32 if index == 0 else BF) for index in range(NX)),
        [SMEM] + [VMEM] * 2,
    )(spot, normed, back)
    travelling = [shift_x(terms[steps], steps) for steps in (2, 1, 3)]

    spare = 16
    sending = call(blocks_kernel, shape((n_dp, features + spare, tokens), BF), [VMEM] * 5)(
        part_own, part_other, inputs_t[:, :tokens], root_mean[:, :tokens], gain_wide
    )
    got = lax.all_to_all(sending, ("y", "h"), 0, 0, tiled=True)
    totals = jnp.sum(got.astype(F32), axis=0)
    own_sums = totals[:features]
    token_totals = totals[features] + totals[features + 1] + totals[features + 2]
    start = lax.axis_index(("y", "h")) * features
    gain_slice = lax.dynamic_slice_in_dim(gain, start, features, 0)[:, None]
    root_own = root_mean[:, :tokens]
    unit_slice = (
        lax.dynamic_slice_in_dim(inputs_t[:, :tokens], start, features, 0).astype(F32) / root_own
    )
    grad_input = (
        ((own_sums * gain_slice - unit_slice * (token_totals / width)[None, :]) / root_own)
        .astype(BF)
        .T
    )
    gain_part = jnp.sum(own_sums * unit_slice, axis=1)
    gain_part, travelling = lax.optimization_barrier((gain_part, travelling))
    grad_gain = lax.psum(lax.psum(gain_part, "x"), ("z", "c"))

    column_sum = call(column_kernel, shape((column_rows, columns), BF), [VMEM] * 4)(
        terms[0], *travelling
    )
    blocks = lax.all_to_all(
        column_sum.reshape(NC * NZ, rows, columns), ("c", "z"), 0, 0, tiled=True
    )
    sums = jnp.sum(blocks.reshape(NC, NZ, rows, columns).astype(F32), axis=1)
    grad_gate = jnp.concatenate([sums[0, :, :half], sums[1, :, :half]], 1)
    grad_up = jnp.concatenate([sums[0, :, half:], sums[1, :, half:]], 1)
    return (hidden, grad_gate, grad_up, grad_input, grad_gain)


def solution(mesh):
    fine = jax.sharding.Mesh(mesh.devices.reshape(NX, NZ, NC, -1, NH), ("x", "z", "c", "y", "h"))
    blk, dp = ("x", "z", "c"), ("y", "h")
    return jax.shard_map(
        per_device,
        mesh=fine,
        in_specs=(P(blk, None), P(), P(blk, dp), P(blk, dp), P(blk, dp)),
        out_specs=(P(blk, dp), P(blk, dp), P(blk, dp), P(blk, dp), P(dp)),
        check_vma=False,
    )
```

```python
import jax
import jax.numpy as jnp
from jax import lax
from jax.experimental import pallas as pl
from jax.experimental.pallas import tpu as pltpu
from jax.sharding import PartitionSpec as P

BF = jnp.bfloat16
F32 = jnp.float32
NX, NZ, NC, NH = 4, 4, 2, 2
VMEM = pl.BlockSpec(memory_space=pltpu.VMEM)
SMEM = pl.BlockSpec(memory_space=pltpu.SMEM)
PARAMS = pltpu.CompilerParams(vmem_limit_bytes=14 * 1024 * 1024)
NT = (((1,), (1,)), ((), ()))
TN = (((0,), (0,)), ((), ()))


def swap(value, axis):
    return lax.ppermute(value, axis, [(0, 1), (1, 0)])


def swap_core(value):
    return swap(value, "c")


def shift_x(value, steps):
    return lax.ppermute(value, "x", [(x, (x + steps) % NX) for x in range(NX)])


def moved(block, core):
    return (block // NZ * NC + core) * NZ + block % NZ


def norm_kernel(x_ref, gain_ref, normed_ref, root_ref):
    width, tokens = x_ref.shape
    size = width // (NX * NZ)
    total = jnp.zeros((size, tokens), F32)
    for index in range(NX * NZ):
        value = x_ref[pl.ds(index * size, size), :].astype(F32)
        total += value * value
    root = jnp.sqrt(jnp.sum(total, axis=0, keepdims=True) / width + 1e-05)
    root_ref[...] = root
    for index in range(NX * NZ):
        rows = pl.ds(index * size, size)
        unit = x_ref[rows, :].astype(F32) / root
        gain = gain_ref[rows, :]
        value = (unit * jnp.concatenate([gain, gain], axis=1)).astype(BF)
        for core in range(NC):
            chunk = size // NC
            normed_ref[pl.ds(moved(index, core) * chunk, chunk), :] = value[
                core * chunk : (core + 1) * chunk
            ]


def forward_kernel(
    normed_ref, upstream_ref, weight_ref, hidden_ref, back_ref, own_ref, other_ref
):
    size = weight_ref.shape[2] // 2
    tokens = own_ref.shape[1]
    width = own_ref.shape[0]

    def piece(index, which):
        return weight_ref[index, :, which * size : (which + 1) * size]

    gate_pre, up_pre = 0.0, 0.0
    for index in range(NX * NC):
        rows = normed_ref[pl.ds(index * size, size), :]
        gate_pre += jnp.dot(piece(index, 0), rows, preferred_element_type=F32)
        up_pre += jnp.dot(piece(index, 1), rows, preferred_element_type=F32)
    sigmoid = 1.0 / (1.0 + jnp.exp(-gate_pre))
    activated = gate_pre * sigmoid
    hidden = activated * up_pre
    hidden_ref[...] = hidden[:, :tokens].astype(BF)
    extra = other_ref.shape[0] - width
    riding = jnp.concatenate(
        [hidden[:, tokens:], jnp.zeros((extra - hidden.shape[0], tokens), F32)], axis=0
    )
    other_ref[width : width + extra, :] = riding.astype(BF)
    upstream = upstream_ref[...].astype(F32)
    back_up = (upstream * activated).astype(BF)
    back_gate = (upstream * up_pre * sigmoid * (1.0 + gate_pre * (1.0 - sigmoid))).astype(BF)
    back_ref[0] = back_gate
    back_ref[1] = back_up
    for index in range(NX * NC):
        part = lax.dot_general(piece(index, 0), back_gate, TN, preferred_element_type=F32)
        part += lax.dot_general(piece(index, 1), back_up, TN, preferred_element_type=F32)
        rows = pl.ds(index * size, size)
        own_ref[rows, :] = part[:, :tokens]
        other_ref[rows, :] = part[:, tokens:].astype(BF)


def gradient_kernel(spot_ref, normed_ref, back_ref, *outs):
    size = outs[0].shape[2]
    for index in range(NX):
        block = (spot_ref[0] + index) % NX
        rows = normed_ref[pl.ds(pl.multiple_of(block * size, size), size), :]
        for which in range(2):
            term = lax.dot_general(back_ref[which], rows, NT, preferred_element_type=F32)
            outs[index][which] = term.astype(outs[index].dtype)


def blocks_kernel(own_ref, other_ref, x_ref, root_ref, gain_ref, out_ref):
    width, tokens = own_ref.shape
    size = width // (NX * NZ)
    root = root_ref[...]
    total = jnp.zeros((size, tokens), F32)
    for index in range(NX * NZ):
        rows = pl.ds(index * size, size)
        chunk = size // NC
        places = [pl.ds(moved(index, core) * chunk, chunk) for core in range(NC)]
        own = jnp.concatenate([own_ref[here, :] for here in places], axis=0)
        other = jnp.concatenate([other_ref[here, :] for here in places], axis=0)
        part = (own + other.astype(F32)).astype(BF)
        out_ref[index, 0:size, :] = part
        unit = x_ref[rows, :].astype(F32) / root
        total += part.astype(F32) * gain_ref[rows, :] * unit
    dots = jnp.sum(total, axis=0, keepdims=True)
    high = dots.astype(BF).astype(F32)
    mid = (dots - high).astype(BF).astype(F32)
    low = dots - high - mid
    spare = out_ref.shape[1] - size
    line = lax.broadcasted_iota(jnp.int32, (spare, tokens), 0)
    rows = jnp.where(line == 0, high, jnp.where(line == 1, mid, jnp.where(line == 2, low, 0.0)))
    for index in range(NX * NZ):
        out_ref[index, size : size + spare, :] = rows.astype(BF)


def column_kernel(own_ref, first_ref, second_ref, third_ref, out_ref):
    half = own_ref.shape[1]
    for which in range(2):
        total = own_ref[which] + first_ref[which].astype(F32)
        total += second_ref[which].astype(F32) + third_ref[which].astype(F32)
        out_ref[:, which * half : (which + 1) * half] = total.T.astype(BF)


def call(kernel, outs, specs):
    return pl.pallas_call(
        kernel,
        out_shape=outs,
        in_specs=specs,
        out_specs=jax.tree.map(lambda _: VMEM, outs),
        compiler_params=PARAMS,
    )


def shape(dims, dtype):
    return jax.ShapeDtypeStruct(dims, dtype)


def per_device(inputs, gain, w_gate, w_up, upstream):
    spot = lax.axis_index("x").astype(jnp.int32).reshape(1)
    first = lax.axis_index("c") == 0
    tokens, width = inputs.shape
    rows, columns = w_gate.shape
    half = columns // 2
    n_dp = lax.axis_size(("y", "h"))
    features = width // n_dp
    column_rows = rows * NZ * NC

    def ordered(own, other, axis):
        return jnp.where(
            first, jnp.concatenate([own, other], axis), jnp.concatenate([other, own], axis)
        )

    def halves(value, axis):
        low, high = jnp.split(value, 2, axis)
        return jnp.where(first, low, high), jnp.where(first, high, low)

    column = lax.all_gather(jnp.concatenate([w_gate, w_up], 1), "z", axis=0, tiled=True).T
    column = jnp.concatenate([column[:columns], column[columns:]], 1)
    copies = jnp.broadcast_to(
        column.reshape(NC, half, column_rows), (NX, NC, half, column_rows)
    ).reshape(NX * NC, half, column_rows)
    weight = lax.all_to_all(copies, ("x", "c"), 0, 0, tiled=True)

    inputs_t = jnp.concatenate([inputs, swap_core(inputs)], 0).T
    upstream_mine, upstream_other = halves(upstream.T, 0)
    upstream_pair = jnp.concatenate([upstream_mine, swap_core(upstream_other)], 1)
    gain_wide = jnp.broadcast_to(gain[:, None], (width, tokens))
    normed, root_mean = call(
        norm_kernel,
        (shape((width, 2 * tokens), BF), shape((1, 2 * tokens), F32)),
        [VMEM] * 2,
    )(inputs_t, gain_wide)

    riding = -(-half // 16) * 16
    hidden_own, back, part_own, part_other = call(
        forward_kernel,
        (
            shape((half, tokens), BF),
            shape((2, half, 2 * tokens), BF),
            shape((width, tokens), F32),
            shape((width + riding, tokens), BF),
        ),
        [VMEM] * 3,
    )(normed, upstream_pair, weight)
    part_other = swap_core(part_other)
    hidden = ordered(hidden_own, part_other[width : width + half], 0).T
    terms = call(
        gradient_kernel,
        tuple(shape((2, half, column_rows), F32 if index == 0 else BF) for index in range(NX)),
        [SMEM] + [VMEM] * 2,
    )(spot, normed, back)
    travelling = [shift_x(terms[steps], steps) for steps in (2, 1, 3)]

    spare = 16
    sending = call(blocks_kernel, shape((n_dp, features + spare, tokens), BF), [VMEM] * 5)(
        part_own, part_other, inputs_t[:, :tokens], root_mean[:, :tokens], gain_wide
    )
    got = lax.all_to_all(sending, ("y", "h"), 0, 0, tiled=True)
    totals = jnp.sum(got.astype(F32), axis=0)
    own_sums = totals[:features]
    token_totals = totals[features] + totals[features + 1] + totals[features + 2]
    start = lax.axis_index(("y", "h")) * features
    gain_slice = lax.dynamic_slice_in_dim(gain, start, features, 0)[:, None]
    root_own = root_mean[:, :tokens]
    unit_slice = (
        lax.dynamic_slice_in_dim(inputs_t[:, :tokens], start, features, 0).astype(F32) / root_own
    )
    grad_input = (
        ((own_sums * gain_slice - unit_slice * (token_totals / width)[None, :]) / root_own)
        .astype(BF)
        .T
    )
    gain_part = jnp.sum(own_sums * unit_slice, axis=1)
    gain_part = lax.psum(gain_part, "x")
    gain_part, travelling = lax.optimization_barrier((gain_part, travelling))
    grad_gain = lax.psum(gain_part, "z")
    grad_gain = grad_gain + swap_core(grad_gain)

    column_sum = call(column_kernel, shape((column_rows, columns), BF), [VMEM] * 4)(
        terms[0], *travelling
    )
    blocks = lax.all_to_all(
        column_sum.reshape(NC * NZ, rows, columns), ("c", "z"), 0, 0, tiled=True
    )
    sums = jnp.sum(blocks.reshape(NC, NZ, rows, columns).astype(F32), axis=1)
    grad_gate = jnp.concatenate([sums[0, :, :half], sums[1, :, :half]], 1)
    grad_up = jnp.concatenate([sums[0, :, half:], sums[1, :, half:]], 1)
    return (hidden, grad_gate, grad_up, grad_input, grad_gain)


def solution(mesh):
    fine = jax.sharding.Mesh(mesh.devices.reshape(NX, NZ, NC, -1, NH), ("x", "z", "c", "y", "h"))
    blk, dp = ("x", "z", "c"), ("y", "h")
    return jax.shard_map(
        per_device,
        mesh=fine,
        in_specs=(P(blk, None), P(), P(blk, dp), P(blk, dp), P(blk, dp)),
        out_specs=(P(blk, dp), P(blk, dp), P(blk, dp), P(blk, dp), P(dp)),
        check_vma=False,
    )
```

```python
import jax
import jax.numpy as jnp
from jax import lax
from jax.experimental import pallas as pl
from jax.experimental.pallas import tpu as pltpu
from jax.sharding import PartitionSpec as P

BF = jnp.bfloat16
F32 = jnp.float32
NX, NZ, NC, NH = 4, 4, 2, 2
ANY = pl.BlockSpec(memory_space=pl.ANY)
VMEM = pl.BlockSpec(memory_space=pltpu.VMEM)
SMEM = pl.BlockSpec(memory_space=pltpu.SMEM)
PARAMS = pltpu.CompilerParams(vmem_limit_bytes=14 * 1024 * 1024)
NT = (((1,), (1,)), ((), ()))
TN = (((0,), (0,)), ((), ()))


def swap(value, axis):
    return lax.ppermute(value, axis, [(0, 1), (1, 0)])


def swap_core(value):
    return swap(value, "c")


def shift_x(value, steps):
    return lax.ppermute(value, "x", [(x, (x + steps) % NX) for x in range(NX)])


def moved(block, core):
    return (block // NZ * NC + core) * NZ + block % NZ


def norm_kernel(x_ref, gain_ref, normed_ref, root_ref):
    width, tokens = x_ref.shape
    size = width // (NX * NZ)
    total = jnp.zeros((size, tokens), F32)
    for index in range(NX * NZ):
        value = x_ref[pl.ds(index * size, size), :].astype(F32)
        total += value * value
    root = jnp.sqrt(jnp.sum(total, axis=0, keepdims=True) / width + 1e-05)
    root_ref[...] = root
    for index in range(NX * NZ):
        rows = pl.ds(index * size, size)
        unit = x_ref[rows, :].astype(F32) / root
        gain = gain_ref[rows, :]
        value = (unit * jnp.concatenate([gain, gain], axis=1)).astype(BF)
        for core in range(NC):
            chunk = size // NC
            normed_ref[pl.ds(moved(index, core) * chunk, chunk), :] = value[
                core * chunk : (core + 1) * chunk
            ]


def forward_kernel(
    normed_from,
    upstream_from,
    weight_ref,
    hidden_ref,
    back_ref,
    own_ref,
    other_ref,
    normed_ref,
    upstream_ref,
    sems,
):
    size = weight_ref.shape[2] // 2
    tokens = own_ref.shape[1]
    width = own_ref.shape[0]
    strip = width // NX
    fetches = [
        pltpu.make_async_copy(
            normed_from.at[pl.ds(index * strip, strip)],
            normed_ref.at[pl.ds(index * strip, strip)],
            sems.at[index],
        )
        for index in range(NX)
    ]
    fetches.append(pltpu.make_async_copy(upstream_from, upstream_ref, sems.at[NX]))
    for fetch in fetches:
        fetch.start()

    def piece(index, which):
        return weight_ref[index, :, which * size : (which + 1) * size]

    gate_pre, up_pre = 0.0, 0.0
    for index in range(NX * NC):
        if index % NC == 0:
            fetches[index // NC].wait()
        rows = normed_ref[pl.ds(index * size, size), :]
        gate_pre += jnp.dot(piece(index, 0), rows, preferred_element_type=F32)
        up_pre += jnp.dot(piece(index, 1), rows, preferred_element_type=F32)
    sigmoid = 1.0 / (1.0 + jnp.exp(-gate_pre))
    activated = gate_pre * sigmoid
    hidden = activated * up_pre
    hidden_ref[...] = hidden[:, :tokens].astype(BF)
    extra = other_ref.shape[0] - width
    riding = jnp.concatenate(
        [hidden[:, tokens:], jnp.zeros((extra - hidden.shape[0], tokens), F32)], axis=0
    )
    other_ref[width : width + extra, :] = riding.astype(BF)
    fetches[NX].wait()
    upstream = upstream_ref[...].astype(F32)
    back_up = (upstream * activated).astype(BF)
    back_gate = (upstream * up_pre * sigmoid * (1.0 + gate_pre * (1.0 - sigmoid))).astype(BF)
    back_ref[0] = back_gate
    back_ref[1] = back_up
    for index in range(NX * NC):
        part = lax.dot_general(piece(index, 0), back_gate, TN, preferred_element_type=F32)
        part += lax.dot_general(piece(index, 1), back_up, TN, preferred_element_type=F32)
        rows = pl.ds(index * size, size)
        own_ref[rows, :] = part[:, :tokens]
        other_ref[rows, :] = part[:, tokens:].astype(BF)


def gradient_kernel(spot_ref, normed_ref, back_ref, *outs):
    size = outs[0].shape[2]
    for index in range(NX):
        block = (spot_ref[0] + index) % NX
        rows = normed_ref[pl.ds(pl.multiple_of(block * size, size), size), :]
        for which in range(2):
            term = lax.dot_general(back_ref[which], rows, NT, preferred_element_type=F32)
            outs[index][which] = term.astype(outs[index].dtype)


def blocks_kernel(
    core_ref, own_ref, other_ref, x_ref, root_ref, gain_ref, mine_ref, out_ref, hidden_ref
):
    width, tokens = own_ref.shape
    half = mine_ref.shape[0]
    mine = mine_ref[...].astype(F32)
    theirs = other_ref[width:, :].astype(F32)[:half]
    first = core_ref[0] == 0
    hidden_ref[...] = jnp.concatenate(
        [jnp.where(first, mine, theirs), jnp.where(first, theirs, mine)], axis=0
    ).astype(BF)
    size = width // (NX * NZ)
    root = root_ref[...]
    total = jnp.zeros((size, tokens), F32)
    for index in range(NX * NZ):
        rows = pl.ds(index * size, size)
        chunk = size // NC
        places = [pl.ds(moved(index, core) * chunk, chunk) for core in range(NC)]
        own = jnp.concatenate([own_ref[here, :] for here in places], axis=0)
        other = jnp.concatenate([other_ref[here, :] for here in places], axis=0)
        part = (own + other.astype(F32)).astype(BF)
        out_ref[index, 0:size, :] = part
        unit = x_ref[rows, :].astype(F32) / root
        total += part.astype(F32) * gain_ref[rows, :] * unit
    dots = jnp.sum(total, axis=0, keepdims=True)
    high = dots.astype(BF).astype(F32)
    mid = (dots - high).astype(BF).astype(F32)
    low = dots - high - mid
    spare = out_ref.shape[1] - size
    line = lax.broadcasted_iota(jnp.int32, (spare, tokens), 0)
    rows = jnp.where(line == 0, high, jnp.where(line == 1, mid, jnp.where(line == 2, low, 0.0)))
    for index in range(NX * NZ):
        out_ref[index, size : size + spare, :] = rows.astype(BF)


def column_kernel(own_ref, first_ref, second_ref, third_ref, out_ref):
    half = own_ref.shape[1]
    for which in range(2):
        total = own_ref[which] + first_ref[which].astype(F32)
        total += second_ref[which].astype(F32) + third_ref[which].astype(F32)
        out_ref[:, which * half : (which + 1) * half] = total.T.astype(BF)


def call(kernel, outs, specs, scratch=()):
    return pl.pallas_call(
        kernel,
        out_shape=outs,
        in_specs=specs,
        scratch_shapes=scratch,
        out_specs=jax.tree.map(lambda _: VMEM, outs),
        compiler_params=PARAMS,
    )


def shape(dims, dtype):
    return jax.ShapeDtypeStruct(dims, dtype)


def per_device(inputs, gain, w_gate, w_up, upstream):
    spot = lax.axis_index("x").astype(jnp.int32).reshape(1)
    first = lax.axis_index("c") == 0
    tokens, width = inputs.shape
    rows, columns = w_gate.shape
    half = columns // 2
    n_dp = lax.axis_size(("y", "h"))
    features = width // n_dp
    column_rows = rows * NZ * NC

    def halves(value, axis):
        low, high = jnp.split(value, 2, axis)
        return jnp.where(first, low, high), jnp.where(first, high, low)

    column = lax.all_gather(jnp.concatenate([w_gate, w_up], 1), "z", axis=0, tiled=True).T
    column = jnp.concatenate([column[:columns], column[columns:]], 1)
    copies = jnp.broadcast_to(
        column.reshape(NC, half, column_rows), (NX, NC, half, column_rows)
    ).reshape(NX * NC, half, column_rows)
    weight = lax.all_to_all(copies, ("x", "c"), 0, 0, tiled=True)

    inputs_t = jnp.concatenate([inputs, swap_core(inputs)], 0).T
    upstream_mine, upstream_other = halves(upstream.T, 0)
    upstream_pair = jnp.concatenate([upstream_mine, swap_core(upstream_other)], 1)
    gain_wide = jnp.broadcast_to(gain[:, None], (width, tokens))
    normed, root_mean = call(
        norm_kernel,
        (shape((width, 2 * tokens), BF), shape((1, 2 * tokens), F32)),
        [VMEM] * 2,
    )(inputs_t, gain_wide)

    riding = -(-half // 16) * 16
    hidden_own, back, part_own, part_other = call(
        forward_kernel,
        (
            shape((half, tokens), BF),
            shape((2, half, 2 * tokens), BF),
            shape((width, tokens), F32),
            shape((width + riding, tokens), BF),
        ),
        [ANY, ANY, VMEM],
        [
            pltpu.VMEM((width, 2 * tokens), BF),
            pltpu.VMEM((half, 2 * tokens), BF),
            pltpu.SemaphoreType.DMA((NX + 1,)),
        ],
    )(normed, upstream_pair, weight)
    part_other = swap_core(part_other)
    terms = call(
        gradient_kernel,
        tuple(shape((2, half, column_rows), F32 if index == 0 else BF) for index in range(NX)),
        [SMEM] + [VMEM] * 2,
    )(spot, normed, back)
    travelling = [shift_x(terms[steps], steps) for steps in (2, 1, 3)]

    spare = 16
    sending, hidden = call(
        blocks_kernel,
        (shape((n_dp, features + spare, tokens), BF), shape((columns, tokens), BF)),
        [SMEM] + [VMEM] * 6,
    )(
        lax.axis_index("c").astype(jnp.int32).reshape(1),
        part_own,
        part_other,
        inputs_t[:, :tokens],
        root_mean[:, :tokens],
        gain_wide,
        hidden_own,
    )
    hidden = hidden.T
    got = lax.all_to_all(sending, ("y", "h"), 0, 0, tiled=True)
    totals = jnp.sum(got.astype(F32), axis=0)
    own_sums = totals[:features]
    token_totals = totals[features] + totals[features + 1] + totals[features + 2]
    start = lax.axis_index(("y", "h")) * features
    gain_slice = lax.dynamic_slice_in_dim(gain, start, features, 0)[:, None]
    root_own = root_mean[:, :tokens]
    unit_slice = (
        lax.dynamic_slice_in_dim(inputs_t[:, :tokens], start, features, 0).astype(F32) / root_own
    )
    grad_input = (
        ((own_sums * gain_slice - unit_slice * (token_totals / width)[None, :]) / root_own)
        .astype(BF)
        .T
    )
    gain_part = jnp.sum(own_sums * unit_slice, axis=1)
    gain_part = lax.psum(gain_part, "z")
    gain_part, travelling = lax.optimization_barrier((gain_part, travelling))
    grad_gain = lax.psum(gain_part, "x")
    grad_gain = grad_gain + swap_core(grad_gain)

    column_sum = call(column_kernel, shape((column_rows, columns), BF), [VMEM] * 4)(
        terms[0], *travelling
    )
    blocks = lax.all_to_all(
        column_sum.reshape(NC * NZ, rows, columns), ("c", "z"), 0, 0, tiled=True
    )
    sums = jnp.sum(blocks.reshape(NC, NZ, rows, columns).astype(F32), axis=1)
    grad_gate = jnp.concatenate([sums[0, :, :half], sums[1, :, :half]], 1)
    grad_up = jnp.concatenate([sums[0, :, half:], sums[1, :, half:]], 1)
    return (hidden, grad_gate, grad_up, grad_input, grad_gain)


def solution(mesh):
    fine = jax.sharding.Mesh(mesh.devices.reshape(NX, NZ, NC, -1, NH), ("x", "z", "c", "y", "h"))
    blk, dp = ("x", "z", "c"), ("y", "h")
    return jax.shard_map(
        per_device,
        mesh=fine,
        in_specs=(P(blk, None), P(), P(blk, dp), P(blk, dp), P(blk, dp)),
        out_specs=(P(blk, dp), P(blk, dp), P(blk, dp), P(blk, dp), P(dp)),
        check_vma=False,
    )
```

```python
import jax
import jax.numpy as jnp
from jax import lax
from jax.experimental import pallas as pl
from jax.experimental.pallas import tpu as pltpu
from jax.sharding import PartitionSpec as P

BF = jnp.bfloat16
F32 = jnp.float32
NX, NZ, NC, NH = 4, 4, 2, 2
VMEM = pl.BlockSpec(memory_space=pltpu.VMEM)
SMEM = pl.BlockSpec(memory_space=pltpu.SMEM)
PARAMS = pltpu.CompilerParams(vmem_limit_bytes=14 * 1024 * 1024)
NT = (((1,), (1,)), ((), ()))
TN = (((0,), (0,)), ((), ()))


def swap(value, axis):
    return lax.ppermute(value, axis, [(0, 1), (1, 0)])


def swap_core(value):
    return swap(value, "c")


def shift_x(value, steps):
    return lax.ppermute(value, "x", [(x, (x + steps) % NX) for x in range(NX)])


def moved(block, core):
    return (block // NZ * NC + core) * NZ + block % NZ


def norm_kernel(x_ref, gain_ref, normed_ref, root_ref):
    width, tokens = x_ref.shape
    size = width // (NX * NZ)
    total = jnp.zeros((size, tokens), F32)
    for index in range(NX * NZ):
        value = x_ref[pl.ds(index * size, size), :].astype(F32)
        total += value * value
    root = jnp.sqrt(jnp.sum(total, axis=0, keepdims=True) / width + 1e-05)
    root_ref[...] = root
    for index in range(NX * NZ):
        rows = pl.ds(index * size, size)
        unit = x_ref[rows, :].astype(F32) / root
        gain = gain_ref[rows, :]
        value = (unit * jnp.concatenate([gain, gain], axis=1)).astype(BF)
        for core in range(NC):
            chunk = size // NC
            normed_ref[pl.ds(moved(index, core) * chunk, chunk), :] = value[
                core * chunk : (core + 1) * chunk
            ]


def forward_kernel(
    normed_ref, upstream_ref, weight_ref, hidden_ref, back_ref, own_ref, other_ref
):
    size = weight_ref.shape[2] // 2
    tokens = own_ref.shape[1]
    width = own_ref.shape[0]

    def piece(index, which):
        return weight_ref[index, :, which * size : (which + 1) * size]

    gate_pre, up_pre = 0.0, 0.0
    for index in range(NX * NC):
        rows = normed_ref[pl.ds(index * size, size), :]
        gate_pre += jnp.dot(piece(index, 0), rows, preferred_element_type=F32)
        up_pre += jnp.dot(piece(index, 1), rows, preferred_element_type=F32)
    sigmoid = 1.0 / (1.0 + jnp.exp(-gate_pre))
    activated = gate_pre * sigmoid
    hidden = activated * up_pre
    hidden_ref[...] = hidden[:, :tokens].astype(BF)
    extra = other_ref.shape[0] - width
    riding = jnp.concatenate(
        [hidden[:, tokens:], jnp.zeros((extra - hidden.shape[0], tokens), F32)], axis=0
    )
    other_ref[width : width + extra, :] = riding.astype(BF)
    upstream = upstream_ref[...].astype(F32)
    back_up = (upstream * activated).astype(BF)
    back_gate = (upstream * up_pre * sigmoid * (1.0 + gate_pre * (1.0 - sigmoid))).astype(BF)
    back_ref[0] = back_gate
    back_ref[1] = back_up
    for index in range(NX * NC):
        part = lax.dot_general(piece(index, 0), back_gate, TN, preferred_element_type=F32)
        part += lax.dot_general(piece(index, 1), back_up, TN, preferred_element_type=F32)
        rows = pl.ds(index * size, size)
        own_ref[rows, :] = part[:, :tokens]
        other_ref[rows, :] = part[:, tokens:].astype(BF)


def gradient_kernel(spot_ref, normed_ref, back_ref, *outs):
    size = outs[0].shape[2]
    for index in range(NX):
        block = (spot_ref[0] + index) % NX
        rows = normed_ref[pl.ds(pl.multiple_of(block * size, size), size), :]
        for which in range(2):
            term = lax.dot_general(back_ref[which], rows, NT, preferred_element_type=F32)
            outs[index][which] = term.astype(outs[index].dtype)


def blocks_kernel(
    core_ref, own_ref, other_ref, x_ref, root_ref, gain_ref, mine_ref, out_ref, hidden_ref
):
    width, tokens = own_ref.shape
    half = mine_ref.shape[0]
    mine = mine_ref[...].astype(F32)
    theirs = other_ref[width:, :].astype(F32)[:half]
    first = core_ref[0] == 0
    hidden_ref[...] = jnp.concatenate(
        [jnp.where(first, mine, theirs), jnp.where(first, theirs, mine)], axis=0
    ).astype(BF)
    size = width // (NX * NZ)
    root = root_ref[...]
    total = jnp.zeros((size, tokens), F32)
    for index in range(NX * NZ):
        rows = pl.ds(index * size, size)
        chunk = size // NC
        places = [pl.ds(moved(index, core) * chunk, chunk) for core in range(NC)]
        own = jnp.concatenate([own_ref[here, :] for here in places], axis=0)
        other = jnp.concatenate([other_ref[here, :] for here in places], axis=0)
        part = (own + other.astype(F32)).astype(BF)
        out_ref[index, 0:size, :] = part
        unit = x_ref[rows, :].astype(F32) / root
        total += part.astype(F32) * gain_ref[rows, :] * unit
    dots = jnp.sum(total, axis=0, keepdims=True)
    high = dots.astype(BF).astype(F32)
    mid = (dots - high).astype(BF).astype(F32)
    low = dots - high - mid
    spare = out_ref.shape[1] - size
    line = lax.broadcasted_iota(jnp.int32, (spare, tokens), 0)
    rows = jnp.where(line == 0, high, jnp.where(line == 1, mid, jnp.where(line == 2, low, 0.0)))
    for index in range(NX * NZ):
        out_ref[index, size : size + spare, :] = rows.astype(BF)


def column_kernel(own_ref, first_ref, second_ref, third_ref, out_ref):
    half = own_ref.shape[1]
    for which in range(2):
        total = own_ref[which] + first_ref[which].astype(F32)
        total += second_ref[which].astype(F32) + third_ref[which].astype(F32)
        out_ref[:, which * half : (which + 1) * half] = total.T.astype(BF)


def call(kernel, outs, specs):
    return pl.pallas_call(
        kernel,
        out_shape=outs,
        in_specs=specs,
        out_specs=jax.tree.map(lambda _: VMEM, outs),
        compiler_params=PARAMS,
    )


def shape(dims, dtype):
    return jax.ShapeDtypeStruct(dims, dtype)


def per_device(inputs, gain, w_gate, w_up, upstream):
    spot = lax.axis_index("x").astype(jnp.int32).reshape(1)
    first = lax.axis_index("c") == 0
    tokens, width = inputs.shape
    rows, columns = w_gate.shape
    half = columns // 2
    n_dp = lax.axis_size(("y", "h"))
    features = width // n_dp
    column_rows = rows * NZ * NC

    def halves(value, axis):
        low, high = jnp.split(value, 2, axis)
        return jnp.where(first, low, high), jnp.where(first, high, low)

    column = lax.all_gather(jnp.concatenate([w_gate, w_up], 1), "z", axis=0, tiled=True).T
    column = jnp.concatenate([column[:columns], column[columns:]], 1)
    copies = jnp.broadcast_to(
        column.reshape(NC, half, column_rows), (NX, NC, half, column_rows)
    ).reshape(NX * NC, half, column_rows)
    weight = lax.all_to_all(copies, ("x", "c"), 0, 0, tiled=True)

    inputs_t = jnp.concatenate([inputs, swap_core(inputs)], 0).T
    upstream_mine, upstream_other = halves(upstream.T, 0)
    upstream_pair = jnp.concatenate([upstream_mine, swap_core(upstream_other)], 1)
    gain_wide = jnp.broadcast_to(gain[:, None], (width, tokens))
    normed, root_mean = call(
        norm_kernel,
        (shape((width, 2 * tokens), BF), shape((1, 2 * tokens), F32)),
        [VMEM] * 2,
    )(inputs_t, gain_wide)

    riding = -(-half // 16) * 16
    hidden_own, back, part_own, part_other = call(
        forward_kernel,
        (
            shape((half, tokens), BF),
            shape((2, half, 2 * tokens), BF),
            shape((width, tokens), F32),
            shape((width + riding, tokens), BF),
        ),
        [VMEM] * 3,
    )(normed, upstream_pair, weight)
    part_other = swap_core(part_other)
    terms = call(
        gradient_kernel,
        tuple(shape((2, half, column_rows), F32 if index == 0 else BF) for index in range(NX)),
        [SMEM] + [VMEM] * 2,
    )(spot, normed, back)
    travelling = [shift_x(terms[steps], steps) for steps in (2, 1, 3)]

    spare = 16
    sending, hidden = call(
        blocks_kernel,
        (shape((n_dp, features + spare, tokens), BF), shape((columns, tokens), BF)),
        [SMEM] + [VMEM] * 6,
    )(
        lax.axis_index("c").astype(jnp.int32).reshape(1),
        part_own,
        part_other,
        inputs_t[:, :tokens],
        root_mean[:, :tokens],
        gain_wide,
        hidden_own,
    )
    hidden = hidden.T
    got = lax.all_to_all(
        sending.reshape(n_dp // NH, NH * (features + spare), tokens), "y", 0, 0, tiled=True
    )
    y_sums = jnp.sum(got.astype(F32), axis=0).reshape(NH, features + spare, tokens)
    root_own = root_mean[:, :tokens]
    tokens_own = inputs_t[:, :tokens]
    span = NH * features
    unit_span = (
        lax.dynamic_slice_in_dim(tokens_own, lax.axis_index("y") * span, span, 0).astype(F32)
        / root_own
    ).reshape(NH, features, tokens)
    gain_part = jnp.sum(y_sums[:, :features] * unit_span, axis=2)
    gain_part = lax.psum(gain_part, ("z", "h"))
    gain_part, travelling = lax.optimization_barrier((gain_part, travelling))
    low_half = lax.axis_index("h") == 0
    gain_part = lax.psum(jnp.where(low_half, gain_part[0], gain_part[1]), "x")
    grad_gain = gain_part + swap_core(gain_part)

    totals = jnp.where(low_half, y_sums[0], y_sums[1]) + swap(
        jnp.where(low_half, y_sums[1], y_sums[0]), "h"
    )
    own_sums = totals[:features]
    token_totals = totals[features] + totals[features + 1] + totals[features + 2]
    start = lax.axis_index(("y", "h")) * features
    gain_slice = lax.dynamic_slice_in_dim(gain, start, features, 0)[:, None]
    unit_slice = jnp.where(low_half, unit_span[0], unit_span[1])
    grad_input = (
        ((own_sums * gain_slice - unit_slice * (token_totals / width)[None, :]) / root_own)
        .astype(BF)
        .T
    )

    column_sum = call(column_kernel, shape((column_rows, columns), BF), [VMEM] * 4)(
        terms[0], *travelling
    )
    blocks = lax.all_to_all(
        column_sum.reshape(NC * NZ, rows, columns), ("c", "z"), 0, 0, tiled=True
    )
    sums = jnp.sum(blocks.reshape(NC, NZ, rows, columns).astype(F32), axis=1)
    grad_gate = jnp.concatenate([sums[0, :, :half], sums[1, :, :half]], 1)
    grad_up = jnp.concatenate([sums[0, :, half:], sums[1, :, half:]], 1)
    return (hidden, grad_gate, grad_up, grad_input, grad_gain)


def solution(mesh):
    fine = jax.sharding.Mesh(mesh.devices.reshape(NX, NZ, NC, -1, NH), ("x", "z", "c", "y", "h"))
    blk, dp = ("x", "z", "c"), ("y", "h")
    return jax.shard_map(
        per_device,
        mesh=fine,
        in_specs=(P(blk, None), P(), P(blk, dp), P(blk, dp), P(blk, dp)),
        out_specs=(P(blk, dp), P(blk, dp), P(blk, dp), P(blk, dp), P(dp)),
        check_vma=False,
    )
```

```python
import jax
import jax.numpy as jnp
from jax import lax
from jax.experimental import pallas as pl
from jax.experimental.pallas import tpu as pltpu
from jax.sharding import PartitionSpec as P

BF = jnp.bfloat16
F32 = jnp.float32
NX, NZ, NC, NH = 4, 4, 2, 2
VMEM = pl.BlockSpec(memory_space=pltpu.VMEM)
SMEM = pl.BlockSpec(memory_space=pltpu.SMEM)
PARAMS = pltpu.CompilerParams(vmem_limit_bytes=14 * 1024 * 1024)
NT = (((1,), (1,)), ((), ()))
TN = (((0,), (0,)), ((), ()))


def swap(value, axis):
    return lax.ppermute(value, axis, [(0, 1), (1, 0)])


def swap_core(value):
    return swap(value, "c")


def shift_x(value, steps):
    return lax.ppermute(value, "x", [(x, (x + steps) % NX) for x in range(NX)])


def moved(block, core):
    return (block // NZ * NC + core) * NZ + block % NZ


def norm_kernel(x_ref, gain_ref, normed_ref, root_ref):
    width, tokens = x_ref.shape
    size = width // (NX * NZ)
    total = jnp.zeros((size, tokens), F32)
    for index in range(NX * NZ):
        value = x_ref[pl.ds(index * size, size), :].astype(F32)
        total += value * value
    root = jnp.sqrt(jnp.sum(total, axis=0, keepdims=True) / width + 1e-05)
    root_ref[...] = root
    for index in range(NX * NZ):
        rows = pl.ds(index * size, size)
        unit = x_ref[rows, :].astype(F32) / root
        gain = gain_ref[rows, :]
        value = (unit * jnp.concatenate([gain, gain], axis=1)).astype(BF)
        for core in range(NC):
            chunk = size // NC
            normed_ref[pl.ds(moved(index, core) * chunk, chunk), :] = value[
                core * chunk : (core + 1) * chunk
            ]


def forward_kernel(
    normed_ref, upstream_ref, weight_ref, hidden_ref, back_ref, own_ref, other_ref
):
    size = weight_ref.shape[2] // 2
    tokens = own_ref.shape[1]
    width = own_ref.shape[0]

    def piece(index, which):
        return weight_ref[index, :, which * size : (which + 1) * size]

    gate_pre, up_pre = 0.0, 0.0
    for index in range(NX * NC):
        rows = normed_ref[pl.ds(index * size, size), :]
        gate_pre += jnp.dot(piece(index, 0), rows, preferred_element_type=F32)
        up_pre += jnp.dot(piece(index, 1), rows, preferred_element_type=F32)
    sigmoid = 1.0 / (1.0 + jnp.exp(-gate_pre))
    activated = gate_pre * sigmoid
    hidden = activated * up_pre
    hidden_ref[...] = hidden[:, :tokens].astype(BF)
    extra = other_ref.shape[0] - width
    riding = jnp.concatenate(
        [hidden[:, tokens:], jnp.zeros((extra - hidden.shape[0], tokens), F32)], axis=0
    )
    other_ref[width : width + extra, :] = riding.astype(BF)
    upstream = upstream_ref[...].astype(F32)
    back_up = (upstream * activated).astype(BF)
    back_gate = (upstream * up_pre * sigmoid * (1.0 + gate_pre * (1.0 - sigmoid))).astype(BF)
    back_ref[0] = back_gate
    back_ref[1] = back_up
    for index in range(NX * NC):
        part = lax.dot_general(piece(index, 0), back_gate, TN, preferred_element_type=F32)
        part += lax.dot_general(piece(index, 1), back_up, TN, preferred_element_type=F32)
        rows = pl.ds(index * size, size)
        own_ref[rows, :] = part[:, :tokens]
        other_ref[rows, :] = part[:, tokens:].astype(BF)


def gradient_kernel(spot_ref, normed_ref, back_ref, *outs):
    size = outs[0].shape[2]
    for index in range(NX):
        block = (spot_ref[0] + index) % NX
        rows = normed_ref[pl.ds(pl.multiple_of(block * size, size), size), :]
        for which in range(2):
            term = lax.dot_general(back_ref[which], rows, NT, preferred_element_type=F32)
            outs[index][which] = term.astype(outs[index].dtype)


def blocks_kernel(
    core_ref, own_ref, other_ref, x_ref, root_ref, gain_ref, mine_ref, out_ref, hidden_ref
):
    width, tokens = own_ref.shape
    half = mine_ref.shape[0]
    mine = mine_ref[...].astype(F32)
    theirs = other_ref[width:, :].astype(F32)[:half]
    first = core_ref[0] == 0
    hidden_ref[...] = jnp.concatenate(
        [jnp.where(first, mine, theirs), jnp.where(first, theirs, mine)], axis=0
    ).astype(BF)
    size = width // (NX * NZ)
    root = root_ref[...]
    total = jnp.zeros((size, tokens), F32)
    for index in range(NX * NZ):
        rows = pl.ds(index * size, size)
        chunk = size // NC
        places = [pl.ds(moved(index, core) * chunk, chunk) for core in range(NC)]
        own = jnp.concatenate([own_ref[here, :] for here in places], axis=0)
        other = jnp.concatenate([other_ref[here, :] for here in places], axis=0)
        part = (own + other.astype(F32)).astype(BF)
        out_ref[index, 0:size, :] = part
        unit = x_ref[rows, :].astype(F32) / root
        total += part.astype(F32) * gain_ref[rows, :] * unit
    dots = jnp.sum(total, axis=0, keepdims=True)
    high = dots.astype(BF).astype(F32)
    mid = (dots - high).astype(BF).astype(F32)
    low = dots - high - mid
    spare = out_ref.shape[1] - size
    line = lax.broadcasted_iota(jnp.int32, (spare, tokens), 0)
    rows = jnp.where(line == 0, high, jnp.where(line == 1, mid, jnp.where(line == 2, low, 0.0)))
    for index in range(NX * NZ):
        out_ref[index, size : size + spare, :] = rows.astype(BF)


def column_kernel(own_ref, first_ref, second_ref, third_ref, out_ref):
    half = own_ref.shape[1]
    for which in range(2):
        total = own_ref[which] + first_ref[which].astype(F32)
        total += second_ref[which].astype(F32) + third_ref[which].astype(F32)
        out_ref[:, which * half : (which + 1) * half] = total.T.astype(BF)


def call(kernel, outs, specs):
    return pl.pallas_call(
        kernel,
        out_shape=outs,
        in_specs=specs,
        out_specs=jax.tree.map(lambda _: VMEM, outs),
        compiler_params=PARAMS,
    )


def shape(dims, dtype):
    return jax.ShapeDtypeStruct(dims, dtype)


def per_device(inputs, gain, w_gate, w_up, upstream):
    spot = lax.axis_index("x").astype(jnp.int32).reshape(1)
    first = lax.axis_index("c") == 0
    tokens, width = inputs.shape
    rows, columns = w_gate.shape
    half = columns // 2
    n_dp = lax.axis_size(("y", "h"))
    features = width // n_dp
    column_rows = rows * NZ * NC

    def halves(value, axis):
        low, high = jnp.split(value, 2, axis)
        return jnp.where(first, low, high), jnp.where(first, high, low)

    column = lax.all_gather(jnp.concatenate([w_gate, w_up], 1), "z", axis=0, tiled=True).T
    column = jnp.concatenate([column[:columns], column[columns:]], 1)
    copies = jnp.broadcast_to(
        column.reshape(NC, half, column_rows), (NX, NC, half, column_rows)
    ).reshape(NX * NC, half, column_rows)
    weight = lax.all_to_all(copies, ("x", "c"), 0, 0, tiled=True)

    inputs_t = jnp.concatenate([inputs, swap_core(inputs)], 0).T
    upstream_mine, upstream_other = halves(upstream.T, 0)
    upstream_pair = jnp.concatenate([upstream_mine, swap_core(upstream_other)], 1)
    gain_wide = jnp.broadcast_to(gain[:, None], (width, tokens))
    normed, root_mean = call(
        norm_kernel,
        (shape((width, 2 * tokens), BF), shape((1, 2 * tokens), F32)),
        [VMEM] * 2,
    )(inputs_t, gain_wide)

    riding = -(-half // 16) * 16
    hidden_own, back, part_own, part_other = call(
        forward_kernel,
        (
            shape((half, tokens), BF),
            shape((2, half, 2 * tokens), BF),
            shape((width, tokens), F32),
            shape((width + riding, tokens), BF),
        ),
        [VMEM] * 3,
    )(normed, upstream_pair, weight)
    part_other = swap_core(part_other)
    terms = call(
        gradient_kernel,
        tuple(shape((2, half, column_rows), F32 if index == 0 else BF) for index in range(NX)),
        [SMEM] + [VMEM] * 2,
    )(spot, normed, back)
    travelling = [shift_x(terms[steps], steps) for steps in (2, 1, 3)]

    spare = 16
    sending, hidden = call(
        blocks_kernel,
        (shape((n_dp, features + spare, tokens), BF), shape((columns, tokens), BF)),
        [SMEM] + [VMEM] * 6,
    )(
        lax.axis_index("c").astype(jnp.int32).reshape(1),
        part_own,
        part_other,
        inputs_t[:, :tokens],
        root_mean[:, :tokens],
        gain_wide,
        hidden_own,
    )
    hidden = hidden.T
    got = lax.all_to_all(
        sending.reshape(n_dp // NH, NH * (features + spare), tokens), "y", 0, 0, tiled=True
    )
    y_sums = jnp.sum(got.astype(F32), axis=0).reshape(NH, features + spare, tokens)
    root_own = root_mean[:, :tokens]
    tokens_own = inputs_t[:, :tokens]
    span = NH * features
    unit_span = (
        lax.dynamic_slice_in_dim(tokens_own, lax.axis_index("y") * span, span, 0).astype(F32)
        / root_own
    ).reshape(NH, features, tokens)
    gain_part = jnp.sum(y_sums[:, :features] * unit_span, axis=2)
    gain_part = lax.psum(gain_part, "z")
    gain_part, travelling = lax.optimization_barrier((gain_part, travelling))

    low_half = lax.axis_index("h") == 0
    lines = -(-features // tokens)
    gain_lines = jnp.pad(gain_part, ((0, 0), (0, lines * tokens - features)))
    y_sums = jnp.concatenate(
        [y_sums[:, : features + 3], gain_lines.reshape(NH, lines, tokens)], 1
    )
    totals = jnp.where(low_half, y_sums[0], y_sums[1]) + swap(
        jnp.where(low_half, y_sums[1], y_sums[0]), "h"
    )
    gain_part = lax.psum(totals[features + 3 :].reshape(lines * tokens)[:features], "x")
    grad_gain = gain_part + swap_core(gain_part)
    own_sums = totals[:features]
    token_totals = totals[features] + totals[features + 1] + totals[features + 2]
    start = lax.axis_index(("y", "h")) * features
    gain_slice = lax.dynamic_slice_in_dim(gain, start, features, 0)[:, None]
    unit_slice = jnp.where(low_half, unit_span[0], unit_span[1])
    grad_input = (
        ((own_sums * gain_slice - unit_slice * (token_totals / width)[None, :]) / root_own)
        .astype(BF)
        .T
    )

    column_sum = call(column_kernel, shape((column_rows, columns), BF), [VMEM] * 4)(
        terms[0], *travelling
    )
    blocks = lax.all_to_all(
        column_sum.reshape(NC * NZ, rows, columns), ("c", "z"), 0, 0, tiled=True
    )
    sums = jnp.sum(blocks.reshape(NC, NZ, rows, columns).astype(F32), axis=1)
    grad_gate = jnp.concatenate([sums[0, :, :half], sums[1, :, :half]], 1)
    grad_up = jnp.concatenate([sums[0, :, half:], sums[1, :, half:]], 1)
    return (hidden, grad_gate, grad_up, grad_input, grad_gain)


def solution(mesh):
    fine = jax.sharding.Mesh(mesh.devices.reshape(NX, NZ, NC, -1, NH), ("x", "z", "c", "y", "h"))
    blk, dp = ("x", "z", "c"), ("y", "h")
    return jax.shard_map(
        per_device,
        mesh=fine,
        in_specs=(P(blk, None), P(), P(blk, dp), P(blk, dp), P(blk, dp)),
        out_specs=(P(blk, dp), P(blk, dp), P(blk, dp), P(blk, dp), P(dp)),
        check_vma=False,
    )
```

```python
import jax
import jax.numpy as jnp
from jax import lax
from jax.experimental import pallas as pl
from jax.experimental.pallas import tpu as pltpu
from jax.sharding import PartitionSpec as P

BF = jnp.bfloat16
F32 = jnp.float32
NX, NZ, NC, NH = 4, 4, 2, 2
VMEM = pl.BlockSpec(memory_space=pltpu.VMEM)
SMEM = pl.BlockSpec(memory_space=pltpu.SMEM)
PARAMS = pltpu.CompilerParams(vmem_limit_bytes=14 * 1024 * 1024)
NT = (((1,), (1,)), ((), ()))
TN = (((0,), (0,)), ((), ()))


def swap(value, axis):
    return lax.ppermute(value, axis, [(0, 1), (1, 0)])


def swap_core(value):
    return swap(value, "c")


def shift_x(value, steps):
    return lax.ppermute(value, "x", [(x, (x + steps) % NX) for x in range(NX)])


def moved(block, core):
    return (block // NZ * NC + core) * NZ + block % NZ


def norm_kernel(x_ref, gain_ref, upstream_ref, normed_ref, root_ref):
    width, tokens = x_ref.shape
    size = width // (NX * NZ)
    half = upstream_ref.shape[0]
    extra = normed_ref.shape[0] - width
    normed_ref[width:, :] = jnp.concatenate(
        [upstream_ref[...].astype(F32), jnp.zeros((extra - half, tokens), F32)], axis=0
    ).astype(BF)
    total = jnp.zeros((size, tokens), F32)
    for index in range(NX * NZ):
        value = x_ref[pl.ds(index * size, size), :].astype(F32)
        total += value * value
    root = jnp.sqrt(jnp.sum(total, axis=0, keepdims=True) / width + 1e-05)
    root_ref[...] = root
    for index in range(NX * NZ):
        rows = pl.ds(index * size, size)
        unit = x_ref[rows, :].astype(F32) / root
        gain = gain_ref[rows, :]
        value = (unit * jnp.concatenate([gain, gain], axis=1)).astype(BF)
        for core in range(NC):
            chunk = size // NC
            normed_ref[pl.ds(moved(index, core) * chunk, chunk), :] = value[
                core * chunk : (core + 1) * chunk
            ]


def forward_kernel(
    normed_ref, weight_ref, hidden_ref, back_ref, own_ref, other_ref
):
    size = weight_ref.shape[2] // 2
    tokens = own_ref.shape[1]
    width = own_ref.shape[0]

    def piece(index, which):
        return weight_ref[index, :, which * size : (which + 1) * size]

    gate_pre, up_pre = 0.0, 0.0
    for index in range(NX * NC):
        rows = normed_ref[pl.ds(index * size, size), :]
        gate_pre += jnp.dot(piece(index, 0), rows, preferred_element_type=F32)
        up_pre += jnp.dot(piece(index, 1), rows, preferred_element_type=F32)
    sigmoid = 1.0 / (1.0 + jnp.exp(-gate_pre))
    activated = gate_pre * sigmoid
    hidden = activated * up_pre
    hidden_ref[...] = hidden[:, :tokens].astype(BF)
    extra = other_ref.shape[0] - width
    riding = jnp.concatenate(
        [hidden[:, tokens:], jnp.zeros((extra - hidden.shape[0], tokens), F32)], axis=0
    )
    other_ref[width : width + extra, :] = riding.astype(BF)
    upstream = normed_ref[width:, :].astype(F32)[: weight_ref.shape[1]]
    back_up = (upstream * activated).astype(BF)
    back_gate = (upstream * up_pre * sigmoid * (1.0 + gate_pre * (1.0 - sigmoid))).astype(BF)
    back_ref[0] = back_gate
    back_ref[1] = back_up
    for index in range(NX * NC):
        part = lax.dot_general(piece(index, 0), back_gate, TN, preferred_element_type=F32)
        part += lax.dot_general(piece(index, 1), back_up, TN, preferred_element_type=F32)
        rows = pl.ds(index * size, size)
        own_ref[rows, :] = part[:, :tokens]
        other_ref[rows, :] = part[:, tokens:].astype(BF)


def gradient_kernel(spot_ref, normed_ref, back_ref, *outs):
    size = outs[0].shape[2]
    for index in range(NX):
        block = (spot_ref[0] + index) % NX
        rows = normed_ref[pl.ds(pl.multiple_of(block * size, size), size), :]
        for which in range(2):
            term = lax.dot_general(back_ref[which], rows, NT, preferred_element_type=F32)
            outs[index][which] = term.astype(outs[index].dtype)


def blocks_kernel(
    core_ref, own_ref, other_ref, x_ref, root_ref, gain_ref, mine_ref, out_ref, hidden_ref
):
    width, tokens = own_ref.shape
    half = mine_ref.shape[0]
    mine = mine_ref[...].astype(F32)
    theirs = other_ref[width:, :].astype(F32)[:half]
    first = core_ref[0] == 0
    hidden_ref[...] = jnp.concatenate(
        [jnp.where(first, mine, theirs), jnp.where(first, theirs, mine)], axis=0
    ).astype(BF)
    size = width // (NX * NZ)
    root = root_ref[...]
    total = jnp.zeros((size, tokens), F32)
    for index in range(NX * NZ):
        rows = pl.ds(index * size, size)
        chunk = size // NC
        places = [pl.ds(moved(index, core) * chunk, chunk) for core in range(NC)]
        own = jnp.concatenate([own_ref[here, :] for here in places], axis=0)
        other = jnp.concatenate([other_ref[here, :] for here in places], axis=0)
        part = (own + other.astype(F32)).astype(BF)
        out_ref[index, 0:size, :] = part
        unit = x_ref[rows, :].astype(F32) / root
        total += part.astype(F32) * gain_ref[rows, :] * unit
    dots = jnp.sum(total, axis=0, keepdims=True)
    high = dots.astype(BF).astype(F32)
    mid = (dots - high).astype(BF).astype(F32)
    low = dots - high - mid
    spare = out_ref.shape[1] - size
    line = lax.broadcasted_iota(jnp.int32, (spare, tokens), 0)
    rows = jnp.where(line == 0, high, jnp.where(line == 1, mid, jnp.where(line == 2, low, 0.0)))
    for index in range(NX * NZ):
        out_ref[index, size : size + spare, :] = rows.astype(BF)


def column_kernel(own_ref, first_ref, second_ref, third_ref, out_ref):
    half = own_ref.shape[1]
    for which in range(2):
        total = own_ref[which] + first_ref[which].astype(F32)
        total += second_ref[which].astype(F32) + third_ref[which].astype(F32)
        out_ref[:, which * half : (which + 1) * half] = total.T.astype(BF)


def call(kernel, outs, specs):
    return pl.pallas_call(
        kernel,
        out_shape=outs,
        in_specs=specs,
        out_specs=jax.tree.map(lambda _: VMEM, outs),
        compiler_params=PARAMS,
    )


def shape(dims, dtype):
    return jax.ShapeDtypeStruct(dims, dtype)


def per_device(inputs, gain, w_gate, w_up, upstream):
    spot = lax.axis_index("x").astype(jnp.int32).reshape(1)
    first = lax.axis_index("c") == 0
    tokens, width = inputs.shape
    rows, columns = w_gate.shape
    half = columns // 2
    n_dp = lax.axis_size(("y", "h"))
    features = width // n_dp
    column_rows = rows * NZ * NC

    def halves(value, axis):
        low, high = jnp.split(value, 2, axis)
        return jnp.where(first, low, high), jnp.where(first, high, low)

    column = lax.all_gather(jnp.concatenate([w_gate, w_up], 1), "z", axis=0, tiled=True).T
    column = jnp.concatenate([column[:columns], column[columns:]], 1)
    copies = jnp.broadcast_to(
        column.reshape(NC, half, column_rows), (NX, NC, half, column_rows)
    ).reshape(NX * NC, half, column_rows)
    weight = lax.all_to_all(copies, ("x", "c"), 0, 0, tiled=True)

    inputs_t = jnp.concatenate([inputs, swap_core(inputs)], 0).T
    upstream_mine, upstream_other = halves(upstream.T, 0)
    upstream_pair = jnp.concatenate([upstream_mine, swap_core(upstream_other)], 1)
    gain_wide = jnp.broadcast_to(gain[:, None], (width, tokens))
    riding = -(-half // 16) * 16
    normed, root_mean = call(
        norm_kernel,
        (shape((width + riding, 2 * tokens), BF), shape((1, 2 * tokens), F32)),
        [VMEM] * 3,
    )(inputs_t, gain_wide, upstream_pair)

    hidden_own, back, part_own, part_other = call(
        forward_kernel,
        (
            shape((half, tokens), BF),
            shape((2, half, 2 * tokens), BF),
            shape((width, tokens), F32),
            shape((width + riding, tokens), BF),
        ),
        [VMEM] * 2,
    )(normed, weight)
    part_other = swap_core(part_other)
    terms = call(
        gradient_kernel,
        tuple(shape((2, half, column_rows), F32 if index == 0 else BF) for index in range(NX)),
        [SMEM] + [VMEM] * 2,
    )(spot, normed, back)
    travelling = [shift_x(terms[steps], steps) for steps in (2, 1, 3)]

    spare = 16
    sending, hidden = call(
        blocks_kernel,
        (shape((n_dp, features + spare, tokens), BF), shape((columns, tokens), BF)),
        [SMEM] + [VMEM] * 6,
    )(
        lax.axis_index("c").astype(jnp.int32).reshape(1),
        part_own,
        part_other,
        inputs_t[:, :tokens],
        root_mean[:, :tokens],
        gain_wide,
        hidden_own,
    )
    hidden = hidden.T
    got = lax.all_to_all(
        sending.reshape(n_dp // NH, NH * (features + spare), tokens), "y", 0, 0, tiled=True
    )
    y_sums = jnp.sum(got.astype(F32), axis=0).reshape(NH, features + spare, tokens)
    root_own = root_mean[:, :tokens]
    tokens_own = inputs_t[:, :tokens]
    span = NH * features
    unit_span = (
        lax.dynamic_slice_in_dim(tokens_own, lax.axis_index("y") * span, span, 0).astype(F32)
        / root_own
    ).reshape(NH, features, tokens)
    gain_part = jnp.sum(y_sums[:, :features] * unit_span, axis=2)
    gain_part = lax.psum(gain_part, "z")
    gain_part, travelling = lax.optimization_barrier((gain_part, travelling))
    column_sum = call(column_kernel, shape((column_rows, columns), BF), [VMEM] * 4)(
        terms[0], *travelling
    )

    low_half = lax.axis_index("h") == 0
    lines = -(-features // tokens)
    gain_lines = jnp.pad(gain_part, ((0, 0), (0, lines * tokens - features)))
    y_sums = jnp.concatenate(
        [y_sums[:, : features + 3], gain_lines.reshape(NH, lines, tokens)], 1
    )
    y_sums, column_sum = lax.optimization_barrier((y_sums, column_sum))
    totals = jnp.where(low_half, y_sums[0], y_sums[1]) + swap(
        jnp.where(low_half, y_sums[1], y_sums[0]), "h"
    )
    gain_part = lax.psum(totals[features + 3 :].reshape(lines * tokens)[:features], "x")
    grad_gain = gain_part + swap_core(gain_part)
    own_sums = totals[:features]
    token_totals = totals[features] + totals[features + 1] + totals[features + 2]
    start = lax.axis_index(("y", "h")) * features
    gain_slice = lax.dynamic_slice_in_dim(gain, start, features, 0)[:, None]
    unit_slice = jnp.where(low_half, unit_span[0], unit_span[1])
    grad_input = (
        ((own_sums * gain_slice - unit_slice * (token_totals / width)[None, :]) / root_own)
        .astype(BF)
        .T
    )

    blocks = lax.all_to_all(
        column_sum.reshape(NC * NZ, rows, columns), ("c", "z"), 0, 0, tiled=True
    )
    sums = jnp.sum(blocks.reshape(NC, NZ, rows, columns).astype(F32), axis=1)
    grad_gate = jnp.concatenate([sums[0, :, :half], sums[1, :, :half]], 1)
    grad_up = jnp.concatenate([sums[0, :, half:], sums[1, :, half:]], 1)
    return (hidden, grad_gate, grad_up, grad_input, grad_gain)


def solution(mesh):
    fine = jax.sharding.Mesh(mesh.devices.reshape(NX, NZ, NC, -1, NH), ("x", "z", "c", "y", "h"))
    blk, dp = ("x", "z", "c"), ("y", "h")
    return jax.shard_map(
        per_device,
        mesh=fine,
        in_specs=(P(blk, None), P(), P(blk, dp), P(blk, dp), P(blk, dp)),
        out_specs=(P(blk, dp), P(blk, dp), P(blk, dp), P(blk, dp), P(dp)),
        check_vma=False,
    )
```

```python
import jax
import jax.numpy as jnp
from jax import lax
from jax.experimental import pallas as pl
from jax.experimental.pallas import tpu as pltpu
from jax.sharding import PartitionSpec as P

BF = jnp.bfloat16
F32 = jnp.float32
NX, NZ, NC, NH = 4, 4, 2, 2
VMEM = pl.BlockSpec(memory_space=pltpu.VMEM)
SMEM = pl.BlockSpec(memory_space=pltpu.SMEM)
PARAMS = pltpu.CompilerParams(vmem_limit_bytes=14 * 1024 * 1024)
NT = (((1,), (1,)), ((), ()))
TN = (((0,), (0,)), ((), ()))


def swap(value, axis):
    return lax.ppermute(value, axis, [(0, 1), (1, 0)])


def swap_core(value):
    return swap(value, "c")


def shift_x(value, steps):
    return lax.ppermute(value, "x", [(x, (x + steps) % NX) for x in range(NX)])


def moved(block, core):
    return (block // NZ * NC + core) * NZ + block % NZ


def norm_kernel(x_ref, gain_ref, upstream_ref, normed_ref, root_ref):
    width, tokens = x_ref.shape
    size = width // (NX * NZ)
    half = upstream_ref.shape[0]
    extra = normed_ref.shape[0] - width
    normed_ref[width:, :] = jnp.concatenate(
        [upstream_ref[...].astype(F32), jnp.zeros((extra - half, tokens), F32)], axis=0
    ).astype(BF)
    total = jnp.zeros((size, tokens), F32)
    for index in range(NX * NZ):
        value = x_ref[pl.ds(index * size, size), :].astype(F32)
        total += value * value
    root = jnp.sqrt(jnp.sum(total, axis=0, keepdims=True) / width + 1e-05)
    root_ref[...] = root
    for index in range(NX * NZ):
        rows = pl.ds(index * size, size)
        unit = x_ref[rows, :].astype(F32) / root
        gain = gain_ref[rows, :]
        value = (unit * jnp.concatenate([gain, gain], axis=1)).astype(BF)
        for core in range(NC):
            chunk = size // NC
            normed_ref[pl.ds(moved(index, core) * chunk, chunk), :] = value[
                core * chunk : (core + 1) * chunk
            ]


def forward_kernel(
    normed_ref, weight_ref, hidden_ref, back_ref, own_ref, other_ref
):
    size = weight_ref.shape[2] // 2
    tokens = own_ref.shape[1]
    width = own_ref.shape[0]

    def piece(index, which):
        return weight_ref[index, :, which * size : (which + 1) * size]

    gate_pre, up_pre = 0.0, 0.0
    for index in range(NX * NC):
        rows = normed_ref[pl.ds(index * size, size), :]
        gate_pre += jnp.dot(piece(index, 0), rows, preferred_element_type=F32)
        up_pre += jnp.dot(piece(index, 1), rows, preferred_element_type=F32)
    sigmoid = 1.0 / (1.0 + jnp.exp(-gate_pre))
    activated = gate_pre * sigmoid
    hidden = activated * up_pre
    hidden_ref[...] = hidden[:, :tokens].astype(BF)
    extra = other_ref.shape[0] - width
    riding = jnp.concatenate(
        [hidden[:, tokens:], jnp.zeros((extra - hidden.shape[0], tokens), F32)], axis=0
    )
    other_ref[width : width + extra, :] = riding.astype(BF)
    upstream = normed_ref[width:, :].astype(F32)[: weight_ref.shape[1]]
    back_up = (upstream * activated).astype(BF)
    back_gate = (upstream * up_pre * sigmoid * (1.0 + gate_pre * (1.0 - sigmoid))).astype(BF)
    back_ref[0] = back_gate
    back_ref[1] = back_up
    for index in range(NX * NC):
        part = lax.dot_general(piece(index, 0), back_gate, TN, preferred_element_type=F32)
        part += lax.dot_general(piece(index, 1), back_up, TN, preferred_element_type=F32)
        rows = pl.ds(index * size, size)
        own_ref[rows, :] = part[:, :tokens]
        other_ref[rows, :] = part[:, tokens:].astype(BF)


def gradient_kernel(spot_ref, normed_ref, back_ref, ready_ref, *outs):
    ready_ref[...] = jnp.zeros_like(ready_ref)
    size = outs[0].shape[2]
    for index in range(NX):
        block = (spot_ref[0] + index) % NX
        rows = normed_ref[pl.ds(pl.multiple_of(block * size, size), size), :]
        for which in range(2):
            term = lax.dot_general(back_ref[which], rows, NT, preferred_element_type=F32)
            outs[index][which] = term.astype(outs[index].dtype)


def blocks_kernel(
    core_ref, _, own_ref, other_ref, x_ref, root_ref, gain_ref, mine_ref, out_ref, hidden_ref
):
    width, tokens = own_ref.shape
    half = mine_ref.shape[0]
    mine = mine_ref[...].astype(F32)
    theirs = other_ref[width:, :].astype(F32)[:half]
    first = core_ref[0] == 0
    hidden_ref[...] = jnp.concatenate(
        [jnp.where(first, mine, theirs), jnp.where(first, theirs, mine)], axis=0
    ).astype(BF)
    size = width // (NX * NZ)
    root = root_ref[...]
    total = jnp.zeros((size, tokens), F32)
    for index in range(NX * NZ):
        rows = pl.ds(index * size, size)
        chunk = size // NC
        places = [pl.ds(moved(index, core) * chunk, chunk) for core in range(NC)]
        own = jnp.concatenate([own_ref[here, :] for here in places], axis=0)
        other = jnp.concatenate([other_ref[here, :] for here in places], axis=0)
        part = (own + other.astype(F32)).astype(BF)
        out_ref[index, 0:size, :] = part
        unit = x_ref[rows, :].astype(F32) / root
        total += part.astype(F32) * gain_ref[rows, :] * unit
    dots = jnp.sum(total, axis=0, keepdims=True)
    high = dots.astype(BF).astype(F32)
    mid = (dots - high).astype(BF).astype(F32)
    low = dots - high - mid
    spare = out_ref.shape[1] - size
    line = lax.broadcasted_iota(jnp.int32, (spare, tokens), 0)
    rows = jnp.where(line == 0, high, jnp.where(line == 1, mid, jnp.where(line == 2, low, 0.0)))
    for index in range(NX * NZ):
        out_ref[index, size : size + spare, :] = rows.astype(BF)


def column_kernel(own_ref, first_ref, second_ref, third_ref, out_ref):
    half = own_ref.shape[1]
    for which in range(2):
        total = own_ref[which] + first_ref[which].astype(F32)
        total += second_ref[which].astype(F32) + third_ref[which].astype(F32)
        out_ref[:, which * half : (which + 1) * half] = total.T.astype(BF)


def call(kernel, outs, specs):
    return pl.pallas_call(
        kernel,
        out_shape=outs,
        in_specs=specs,
        out_specs=jax.tree.map(lambda _: VMEM, outs),
        compiler_params=PARAMS,
    )


def shape(dims, dtype):
    return jax.ShapeDtypeStruct(dims, dtype)


def per_device(inputs, gain, w_gate, w_up, upstream):
    spot = lax.axis_index("x").astype(jnp.int32).reshape(1)
    first = lax.axis_index("c") == 0
    tokens, width = inputs.shape
    rows, columns = w_gate.shape
    half = columns // 2
    n_dp = lax.axis_size(("y", "h"))
    features = width // n_dp
    column_rows = rows * NZ * NC

    def halves(value, axis):
        low, high = jnp.split(value, 2, axis)
        return jnp.where(first, low, high), jnp.where(first, high, low)

    column = lax.all_gather(jnp.concatenate([w_gate, w_up], 1), "z", axis=0, tiled=True).T
    column = jnp.concatenate([column[:columns], column[columns:]], 1)
    copies = jnp.broadcast_to(
        column.reshape(NC, half, column_rows), (NX, NC, half, column_rows)
    ).reshape(NX * NC, half, column_rows)
    weight = lax.all_to_all(copies, ("x", "c"), 0, 0, tiled=True)

    inputs_t = jnp.concatenate([inputs, swap_core(inputs)], 0).T
    upstream_mine, upstream_other = halves(upstream.T, 0)
    upstream_pair = jnp.concatenate([upstream_mine, swap_core(upstream_other)], 1)
    gain_wide = jnp.broadcast_to(gain[:, None], (width, tokens))
    riding = -(-half // 16) * 16
    normed, root_mean = call(
        norm_kernel,
        (shape((width + riding, 2 * tokens), BF), shape((1, 2 * tokens), F32)),
        [VMEM] * 3,
    )(inputs_t, gain_wide, upstream_pair)

    hidden_own, back, part_own, part_other = call(
        forward_kernel,
        (
            shape((half, tokens), BF),
            shape((2, half, 2 * tokens), BF),
            shape((width, tokens), F32),
            shape((width + riding, tokens), BF),
        ),
        [VMEM] * 2,
    )(normed, weight)
    part_other = swap_core(part_other)
    ready, *terms = call(
        gradient_kernel,
        (shape((8, 128), F32),)
        + tuple(shape((2, half, column_rows), F32 if index == 0 else BF) for index in range(NX)),
        [SMEM] + [VMEM] * 2,
    )(spot, normed, back)
    travelling = [shift_x(terms[steps], steps) for steps in (2, 1, 3)]

    spare = 16
    sending, hidden = call(
        blocks_kernel,
        (shape((n_dp, features + spare, tokens), BF), shape((columns, tokens), BF)),
        [SMEM] + [VMEM] * 7,
    )(
        lax.axis_index("c").astype(jnp.int32).reshape(1),
        ready,
        part_own,
        part_other,
        inputs_t[:, :tokens],
        root_mean[:, :tokens],
        gain_wide,
        hidden_own,
    )
    hidden = hidden.T
    got = lax.all_to_all(
        sending.reshape(n_dp // NH, NH * (features + spare), tokens), "y", 0, 0, tiled=True
    )
    y_sums = jnp.sum(got.astype(F32), axis=0).reshape(NH, features + spare, tokens)
    root_own = root_mean[:, :tokens]
    tokens_own = inputs_t[:, :tokens]
    span = NH * features
    unit_span = (
        lax.dynamic_slice_in_dim(tokens_own, lax.axis_index("y") * span, span, 0).astype(F32)
        / root_own
    ).reshape(NH, features, tokens)
    gain_part = jnp.sum(y_sums[:, :features] * unit_span, axis=2)
    gain_part = lax.psum(gain_part, "z")
    gain_part, travelling = lax.optimization_barrier((gain_part, travelling))
    column_sum = call(column_kernel, shape((column_rows, columns), BF), [VMEM] * 4)(
        terms[0], *travelling
    )

    low_half = lax.axis_index("h") == 0
    lines = -(-features // tokens)
    gain_lines = jnp.pad(gain_part, ((0, 0), (0, lines * tokens - features)))
    y_sums = jnp.concatenate(
        [y_sums[:, : features + 3], gain_lines.reshape(NH, lines, tokens)], 1
    )
    y_sums, column_sum = lax.optimization_barrier((y_sums, column_sum))
    totals = jnp.where(low_half, y_sums[0], y_sums[1]) + swap(
        jnp.where(low_half, y_sums[1], y_sums[0]), "h"
    )
    gain_part = lax.psum(totals[features + 3 :].reshape(lines * tokens)[:features], "x")
    grad_gain = gain_part + swap_core(gain_part)
    own_sums = totals[:features]
    token_totals = totals[features] + totals[features + 1] + totals[features + 2]
    start = lax.axis_index(("y", "h")) * features
    gain_slice = lax.dynamic_slice_in_dim(gain, start, features, 0)[:, None]
    unit_slice = jnp.where(low_half, unit_span[0], unit_span[1])
    grad_input = (
        ((own_sums * gain_slice - unit_slice * (token_totals / width)[None, :]) / root_own)
        .astype(BF)
        .T
    )

    blocks = lax.all_to_all(
        column_sum.reshape(NC * NZ, rows, columns), ("c", "z"), 0, 0, tiled=True
    )
    sums = jnp.sum(blocks.reshape(NC, NZ, rows, columns).astype(F32), axis=1)
    grad_gate = jnp.concatenate([sums[0, :, :half], sums[1, :, :half]], 1)
    grad_up = jnp.concatenate([sums[0, :, half:], sums[1, :, half:]], 1)
    return (hidden, grad_gate, grad_up, grad_input, grad_gain)


def solution(mesh):
    fine = jax.sharding.Mesh(mesh.devices.reshape(NX, NZ, NC, -1, NH), ("x", "z", "c", "y", "h"))
    blk, dp = ("x", "z", "c"), ("y", "h")
    return jax.shard_map(
        per_device,
        mesh=fine,
        in_specs=(P(blk, None), P(), P(blk, dp), P(blk, dp), P(blk, dp)),
        out_specs=(P(blk, dp), P(blk, dp), P(blk, dp), P(blk, dp), P(dp)),
        check_vma=False,
    )
```

```python
import functools

import jax
import jax.numpy as jnp
from jax import lax
from jax.experimental import pallas as pl
from jax.experimental.pallas import tpu as pltpu
from jax.sharding import PartitionSpec as P

BF = jnp.bfloat16
F32 = jnp.float32
NX, NZ, NC, NH = 4, 4, 2, 2
VMEM = pl.BlockSpec(memory_space=pltpu.VMEM)
SMEM = pl.BlockSpec(memory_space=pltpu.SMEM)
PARAMS = pltpu.CompilerParams(vmem_limit_bytes=14 * 1024 * 1024)
NT = (((1,), (1,)), ((), ()))
TN = (((0,), (0,)), ((), ()))


def swap(value, axis):
    return lax.ppermute(value, axis, [(0, 1), (1, 0)])


def swap_core(value):
    return swap(value, "c")


def shift_x(value, steps):
    return lax.ppermute(value, "x", [(x, (x + steps) % NX) for x in range(NX)])


def moved(block, core):
    return (block // NZ * NC + core) * NZ + block % NZ


def norm_kernel(x_ref, gain_ref, upstream_ref, normed_ref, root_ref):
    width, tokens = x_ref.shape
    size = width // (NX * NZ)
    half = upstream_ref.shape[0]
    extra = normed_ref.shape[0] - width
    normed_ref[width:, :] = jnp.concatenate(
        [upstream_ref[...].astype(F32), jnp.zeros((extra - half, tokens), F32)], axis=0
    ).astype(BF)
    total = jnp.zeros((size, tokens), F32)
    for index in range(NX * NZ):
        value = x_ref[pl.ds(index * size, size), :].astype(F32)
        total += value * value
    root = jnp.sqrt(jnp.sum(total, axis=0, keepdims=True) / width + 1e-05)
    root_ref[...] = root
    for index in range(NX * NZ):
        rows = pl.ds(index * size, size)
        unit = x_ref[rows, :].astype(F32) / root
        gain = gain_ref[rows, :]
        value = (unit * jnp.concatenate([gain, gain], axis=1)).astype(BF)
        for core in range(NC):
            chunk = size // NC
            normed_ref[pl.ds(moved(index, core) * chunk, chunk), :] = value[
                core * chunk : (core + 1) * chunk
            ]


def forward_kernel(
    normed_ref, weight_ref, hidden_ref, back_ref, own_ref, other_ref
):
    size = weight_ref.shape[2] // 2
    tokens = own_ref.shape[1]
    width = own_ref.shape[0]

    def piece(index, which):
        return weight_ref[index, :, which * size : (which + 1) * size]

    gate_pre, up_pre = 0.0, 0.0
    for index in range(NX * NC):
        rows = normed_ref[pl.ds(index * size, size), :]
        gate_pre += jnp.dot(piece(index, 0), rows, preferred_element_type=F32)
        up_pre += jnp.dot(piece(index, 1), rows, preferred_element_type=F32)
    sigmoid = 1.0 / (1.0 + jnp.exp(-gate_pre))
    activated = gate_pre * sigmoid
    hidden = activated * up_pre
    hidden_ref[...] = hidden[:, :tokens].astype(BF)
    extra = other_ref.shape[0] - width
    riding = jnp.concatenate(
        [hidden[:, tokens:], jnp.zeros((extra - hidden.shape[0], tokens), F32)], axis=0
    )
    other_ref[width : width + extra, :] = riding.astype(BF)
    upstream = normed_ref[width:, :].astype(F32)[: weight_ref.shape[1]]
    back_up = (upstream * activated).astype(BF)
    back_gate = (upstream * up_pre * sigmoid * (1.0 + gate_pre * (1.0 - sigmoid))).astype(BF)
    back_ref[0] = back_gate
    back_ref[1] = back_up
    for index in range(NX * NC):
        part = lax.dot_general(piece(index, 0), back_gate, TN, preferred_element_type=F32)
        part += lax.dot_general(piece(index, 1), back_up, TN, preferred_element_type=F32)
        rows = pl.ds(index * size, size)
        own_ref[rows, :] = part[:, :tokens]
        other_ref[rows, :] = part[:, tokens:].astype(BF)


def gradient_kernel(steps, spot_ref, normed_ref, back_ref, *outs):
    size = outs[0].shape[2]
    for index, step in enumerate(steps):
        block = (spot_ref[0] + step) % NX
        rows = normed_ref[pl.ds(pl.multiple_of(block * size, size), size), :]
        for which in range(2):
            term = lax.dot_general(back_ref[which], rows, NT, preferred_element_type=F32)
            outs[index][which] = term.astype(outs[index].dtype)


def blocks_kernel(
    core_ref, own_ref, other_ref, x_ref, root_ref, gain_ref, mine_ref, out_ref, hidden_ref
):
    width, tokens = own_ref.shape
    half = mine_ref.shape[0]
    mine = mine_ref[...].astype(F32)
    theirs = other_ref[width:, :].astype(F32)[:half]
    first = core_ref[0] == 0
    hidden_ref[...] = jnp.concatenate(
        [jnp.where(first, mine, theirs), jnp.where(first, theirs, mine)], axis=0
    ).astype(BF)
    size = width // (NX * NZ)
    root = root_ref[...]
    total = jnp.zeros((size, tokens), F32)
    for index in range(NX * NZ):
        rows = pl.ds(index * size, size)
        chunk = size // NC
        places = [pl.ds(moved(index, core) * chunk, chunk) for core in range(NC)]
        own = jnp.concatenate([own_ref[here, :] for here in places], axis=0)
        other = jnp.concatenate([other_ref[here, :] for here in places], axis=0)
        part = (own + other.astype(F32)).astype(BF)
        out_ref[index, 0:size, :] = part
        unit = x_ref[rows, :].astype(F32) / root
        total += part.astype(F32) * gain_ref[rows, :] * unit
    dots = jnp.sum(total, axis=0, keepdims=True)
    high = dots.astype(BF).astype(F32)
    mid = (dots - high).astype(BF).astype(F32)
    low = dots - high - mid
    spare = out_ref.shape[1] - size
    line = lax.broadcasted_iota(jnp.int32, (spare, tokens), 0)
    rows = jnp.where(line == 0, high, jnp.where(line == 1, mid, jnp.where(line == 2, low, 0.0)))
    for index in range(NX * NZ):
        out_ref[index, size : size + spare, :] = rows.astype(BF)


def column_kernel(own_ref, first_ref, second_ref, third_ref, out_ref):
    half = own_ref.shape[1]
    for which in range(2):
        total = own_ref[which] + first_ref[which].astype(F32)
        total += second_ref[which].astype(F32) + third_ref[which].astype(F32)
        out_ref[:, which * half : (which + 1) * half] = total.T.astype(BF)


def call(kernel, outs, specs):
    return pl.pallas_call(
        kernel,
        out_shape=outs,
        in_specs=specs,
        out_specs=jax.tree.map(lambda _: VMEM, outs),
        compiler_params=PARAMS,
    )


def shape(dims, dtype):
    return jax.ShapeDtypeStruct(dims, dtype)


def per_device(inputs, gain, w_gate, w_up, upstream):
    spot = lax.axis_index("x").astype(jnp.int32).reshape(1)
    first = lax.axis_index("c") == 0
    tokens, width = inputs.shape
    rows, columns = w_gate.shape
    half = columns // 2
    n_dp = lax.axis_size(("y", "h"))
    features = width // n_dp
    column_rows = rows * NZ * NC

    def halves(value, axis):
        low, high = jnp.split(value, 2, axis)
        return jnp.where(first, low, high), jnp.where(first, high, low)

    column = lax.all_gather(jnp.concatenate([w_gate, w_up], 1), "z", axis=0, tiled=True).T
    column = jnp.concatenate([column[:columns], column[columns:]], 1)
    copies = jnp.broadcast_to(
        column.reshape(NC, half, column_rows), (NX, NC, half, column_rows)
    ).reshape(NX * NC, half, column_rows)
    weight = lax.all_to_all(copies, ("x", "c"), 0, 0, tiled=True)

    inputs_t = jnp.concatenate([inputs, swap_core(inputs)], 0).T
    upstream_mine, upstream_other = halves(upstream.T, 0)
    upstream_pair = jnp.concatenate([upstream_mine, swap_core(upstream_other)], 1)
    gain_wide = jnp.broadcast_to(gain[:, None], (width, tokens))
    riding = -(-half // 16) * 16
    normed, root_mean = call(
        norm_kernel,
        (shape((width + riding, 2 * tokens), BF), shape((1, 2 * tokens), F32)),
        [VMEM] * 3,
    )(inputs_t, gain_wide, upstream_pair)

    hidden_own, back, part_own, part_other = call(
        forward_kernel,
        (
            shape((half, tokens), BF),
            shape((2, half, 2 * tokens), BF),
            shape((width, tokens), F32),
            shape((width + riding, tokens), BF),
        ),
        [VMEM] * 2,
    )(normed, weight)
    part_other = swap_core(part_other)
    def gradient(steps, dtype):
        return call(
            functools.partial(gradient_kernel, steps),
            tuple(shape((2, half, column_rows), dtype) for _ in steps),
            [SMEM] + [VMEM] * 2,
        )(spot, normed, back)

    (far,) = gradient((2,), BF)
    after, before = gradient((1, 3), BF)
    (own_term,) = gradient((0,), F32)
    travelling = [shift_x(far, 2), shift_x(after, 1), shift_x(before, 3)]

    spare = 16
    sending, hidden = call(
        blocks_kernel,
        (shape((n_dp, features + spare, tokens), BF), shape((columns, tokens), BF)),
        [SMEM] + [VMEM] * 6,
    )(
        lax.axis_index("c").astype(jnp.int32).reshape(1),
        part_own,
        part_other,
        inputs_t[:, :tokens],
        root_mean[:, :tokens],
        gain_wide,
        hidden_own,
    )
    hidden = hidden.T
    got = lax.all_to_all(
        sending.reshape(n_dp // NH, NH * (features + spare), tokens), "y", 0, 0, tiled=True
    )
    y_sums = jnp.sum(got.astype(F32), axis=0).reshape(NH, features + spare, tokens)
    root_own = root_mean[:, :tokens]
    tokens_own = inputs_t[:, :tokens]
    span = NH * features
    unit_span = (
        lax.dynamic_slice_in_dim(tokens_own, lax.axis_index("y") * span, span, 0).astype(F32)
        / root_own
    ).reshape(NH, features, tokens)
    gain_part = jnp.sum(y_sums[:, :features] * unit_span, axis=2)
    gain_part = lax.psum(gain_part, "z")
    gain_part, travelling = lax.optimization_barrier((gain_part, travelling))
    column_sum = call(column_kernel, shape((column_rows, columns), BF), [VMEM] * 4)(
        own_term, *travelling
    )

    low_half = lax.axis_index("h") == 0
    lines = -(-features // tokens)
    gain_lines = jnp.pad(gain_part, ((0, 0), (0, lines * tokens - features)))
    y_sums = jnp.concatenate(
        [y_sums[:, : features + 3], gain_lines.reshape(NH, lines, tokens)], 1
    )
    y_sums, column_sum = lax.optimization_barrier((y_sums, column_sum))
    totals = jnp.where(low_half, y_sums[0], y_sums[1]) + swap(
        jnp.where(low_half, y_sums[1], y_sums[0]), "h"
    )
    gain_part = lax.psum(totals[features + 3 :].reshape(lines * tokens)[:features], "x")
    grad_gain = gain_part + swap_core(gain_part)
    own_sums = totals[:features]
    token_totals = totals[features] + totals[features + 1] + totals[features + 2]
    start = lax.axis_index(("y", "h")) * features
    gain_slice = lax.dynamic_slice_in_dim(gain, start, features, 0)[:, None]
    unit_slice = jnp.where(low_half, unit_span[0], unit_span[1])
    grad_input = (
        ((own_sums * gain_slice - unit_slice * (token_totals / width)[None, :]) / root_own)
        .astype(BF)
        .T
    )

    blocks = lax.all_to_all(
        column_sum.reshape(NC * NZ, rows, columns), ("c", "z"), 0, 0, tiled=True
    )
    sums = jnp.sum(blocks.reshape(NC, NZ, rows, columns).astype(F32), axis=1)
    grad_gate = jnp.concatenate([sums[0, :, :half], sums[1, :, :half]], 1)
    grad_up = jnp.concatenate([sums[0, :, half:], sums[1, :, half:]], 1)
    return (hidden, grad_gate, grad_up, grad_input, grad_gain)


def solution(mesh):
    fine = jax.sharding.Mesh(mesh.devices.reshape(NX, NZ, NC, -1, NH), ("x", "z", "c", "y", "h"))
    blk, dp = ("x", "z", "c"), ("y", "h")
    return jax.shard_map(
        per_device,
        mesh=fine,
        in_specs=(P(blk, None), P(), P(blk, dp), P(blk, dp), P(blk, dp)),
        out_specs=(P(blk, dp), P(blk, dp), P(blk, dp), P(blk, dp), P(dp)),
        check_vma=False,
    )
```
